32 devices in a mesh: grp: 4 (over y, x), tile: 8 (over z, core).
Axes of the slice: x: 2, y: 2, z: 4, core: 2. Of those that a mesh axis runs over, the one named last changes fastest.
Arguments:
- screens: bfloat16 [3, 32768, 256], P(None, ('grp', 'tile')), may hold values from -4 to 4
- interp_weights: bfloat16 [3, 4, 256, 256], replicated, may hold values from -0.375 to 0.375
- footprint: int32 [8192, 3, 4], P(('grp', 'tile')), may hold values from 0 to 32767, as said below
- illumination: float32 [8192, 256], P(('grp', 'tile')), may hold values from 0.3 to 1
- cm_values: bfloat16 [896, 16, 16, 2, 128], P('tile', 'grp'), may hold values from -0.09375 to 0.09375
- cm_columns: int32 [896, 16], P('tile', 'grp'), may hold values from 0 to 63, as said below
- prev_commands: float32 [14336], P('tile'), may hold values from 0 to 5
- owner_map: int32 [14336], P('tile'), may hold values from 0 to 2, as said below
- dm_gain: float32 [3], replicated, may hold values from 0.2 to 1
Outputs:
- slopes: float32 [2, 8192], P(None, ('grp', 'tile'))
- commands: float32 [14336], P('tile')
The draws below stay inside these ranges and needn't reach their ends.
Inputs may be any that keep to these rules, and one draw needn't show every extreme that they name: `footprint`: the blocks of subaperture s lie among the 1024 blocks of the device holding s and the 256 blocks on either side of them, counted cyclically over all 32768 blocks; some subaperture reaches each end. `cm_columns`: nonzero block n names a column block from (n // 4) * 16 up to that plus 16 - 1. `owner_map`: every mirror owns some actuator.
All inputs are finite; a program needn't handle non-finite values.
Results may differ from the reference program's by a relative error of at most 0.0024.
Values may be sent and summed in bfloat16 or wider, within the bound.
A program may use at most 64 MiB of HBM per device.

```python
import math
import jax
import jax.numpy as jnp
from jax import lax

SIDE = 16
P_SIZE = 256
LAYERS = 3
FOOT = 4
SUB_DEV = 256
BLK_DEV = 1024
REACH = 256
SUBS = 8192
SBLK = 32768
CBS = 128
NCB = 64
NCB_GRP = 16
RB = 16
ACT = 14336
ROWBLK = 896
NZB = 16
NZ_GRP = 4
NDM = 3


def draw_footprint(key, part):
    offsets = jax.random.randint(key, (SUBS, LAYERS, FOOT), -REACH, BLK_DEV + REACH)
    subap = jnp.arange(SUBS, dtype=jnp.int32)[:, None, None]
    owner = subap // SUB_DEV
    layer_ids = jnp.arange(LAYERS, dtype=jnp.int32)[None, :, None]
    slot_ids = jnp.arange(FOOT, dtype=jnp.int32)[None, None, :]
    forced = jnp.where(slot_ids == 0, -REACH, jnp.where(slot_ids == 1, BLK_DEV + REACH - 1, jnp.where(slot_ids == 2, -1, BLK_DEV)))
    first = (subap % SUB_DEV == 0) & (layer_ids == 0)
    offsets = jnp.where(first, forced, offsets)
    return ((owner * BLK_DEV + offsets) % SBLK).astype(jnp.int32)


def draw_cm_columns(key, part):
    picks = jax.random.randint(key, (ROWBLK, NZB), 0, NCB_GRP)
    group_ids = jnp.arange(NZB, dtype=jnp.int32)[None, :] // NZ_GRP
    columns = group_ids * NCB_GRP + picks
    rows = jnp.arange(ROWBLK, dtype=jnp.int32)[:, None]
    slots = jnp.arange(NZB, dtype=jnp.int32)[None, :]
    columns = jnp.where((rows == 0) & (slots == 0), 0, columns)
    columns = jnp.where((rows == 0) & (slots == NZB - 1), NCB - 1, columns)
    return columns.astype(jnp.int32)


def draw_owner_map(key, part):
    owners = jax.random.randint(key, (ACT,), 0, NDM)
    index = jnp.arange(ACT, dtype=jnp.int32)
    owners = jnp.where(index < NDM, index, owners)
    return owners.astype(jnp.int32)


def draw_prev_commands(key, part):
    ramp = 1.0 + 2.0 * jnp.arange(ACT, dtype=jnp.float32) / ACT
    values = jax.random.uniform(key, (ACT,), jnp.float32, 0.5, 1.5) * ramp
    return values.astype(jnp.float32)


def steps_of(own_key, dims, shards, smallest, largest):
    level, own = 1.0, jax.random.fold_in(own_key, 6)
    for position, blocks in shards:
        heights = jnp.exp(jax.random.uniform(jax.random.fold_in(own, position), (blocks,), jnp.float32, smallest / len(shards), largest / len(shards)))
        level = level * jnp.repeat(heights, dims[position] // blocks).reshape([-1 if axis == position else 1 for axis in range(len(dims))])
    return level


def gaussian(own_key, extent, deviation, bound, shards=(), kind=jnp.bfloat16):
    level = steps_of(own_key, extent, shards, -0.22, 0.18) if shards else 1.0
    result = jax.random.normal(own_key, extent, jnp.float32) * deviation * level
    return jnp.minimum(jnp.maximum(result, -bound), bound).astype(kind)


def setup_inputs(seed: int = 0) -> dict:
    seeds = jax.random.split(jax.random.key(seed), 10)
    screens = gaussian(seeds[0], (LAYERS, SBLK, P_SIZE), 0.5, 4.0, ((1, 32),))
    interp_weights = gaussian(seeds[1], (LAYERS, FOOT, P_SIZE, P_SIZE), P_SIZE ** -0.5, 0.375)
    footprint = draw_footprint(jax.random.fold_in(seeds[9], 71), 0)
    illumination = jnp.clip(jnp.exp(math.log(1.0) - 1.2039728 * jax.random.uniform(seeds[3], (SUBS, P_SIZE), jnp.float32) ** steps_of(seeds[3], (SUBS, P_SIZE), ((0, 32),), -0.2, 0.2)), 0.3, 1.0)
    cm_values = gaussian(seeds[4], (ROWBLK, NZB, RB, 2, CBS), (NZB * 2 * CBS) ** -0.5, 0.09375, ((0, 8), (1, 4)))
    cm_columns = draw_cm_columns(jax.random.fold_in(seeds[9], 71), 0)
    prev_commands = draw_prev_commands(jax.random.fold_in(seeds[9], 71), 0)
    owner_map = draw_owner_map(jax.random.fold_in(seeds[9], 71), 0)
    dm_gain = jnp.clip(jnp.exp(jax.random.uniform(seeds[8], (NDM,), jnp.float32, math.log(0.2), math.log(1.0))), 0.2, 1.0)
    return {"screens": screens, "interp_weights": interp_weights, "footprint": footprint, "illumination": illumination, "cm_values": cm_values, "cm_columns": cm_columns, "prev_commands": prev_commands, "owner_map": owner_map, "dm_gain": dm_gain}


def spectrum_tables(side):
    pixels = side * side
    index = jnp.arange(pixels, dtype=jnp.int32)
    row_ids = index // side
    col_ids = index % side
    turns = (row_ids[:, None] * row_ids[None, :] + col_ids[:, None] * col_ids[None, :]) % side
    angle = turns.astype(jnp.float32) * (2.0 * math.pi / side)
    cosine = jnp.cos(angle)
    sine = jnp.sin(angle)
    table = jnp.concatenate([jnp.concatenate([cosine, -sine], 1), jnp.concatenate([sine, cosine], 1)], 0)
    half = side // 2
    centre_v = (col_ids - side * (col_ids >= half).astype(jnp.int32)).astype(jnp.float32)
    centre_u = (row_ids - side * (row_ids >= half).astype(jnp.int32)).astype(jnp.float32)
    return table.astype(jnp.bfloat16), centre_v, centre_u


def spot_slopes(phase, illum, table, centre_v, centre_u):
    pixels = phase.shape[1]
    field = jnp.concatenate([illum * jnp.cos(phase), illum * jnp.sin(phase)], 1).astype(jnp.bfloat16)
    spectrum = jnp.dot(field, table, preferred_element_type=jnp.float32)
    real_part = spectrum[:, :pixels]
    imag_part = spectrum[:, pixels:]
    intensity = real_part * real_part + imag_part * imag_part
    total = jnp.sum(intensity, axis=1)
    slope_x = jnp.sum(intensity * centre_v[None, :], axis=1) / total
    slope_y = jnp.sum(intensity * centre_u[None, :], axis=1) / total
    return jnp.stack([slope_x, slope_y], 0)


def settle(recon, prev_commands, owner_map, dm_gain):
    mirrors = dm_gain.shape[0]
    onehot = (owner_map[:, None] == jnp.arange(mirrors, dtype=jnp.int32)[None, :]).astype(jnp.float32)
    gains = jnp.sum(onehot * dm_gain[None, :], axis=1)
    updated = prev_commands - gains * recon
    sums = jnp.sum(onehot * updated[:, None], axis=0)
    counts = jnp.sum(onehot, axis=0)
    piston = sums / counts
    return updated - jnp.sum(onehot * piston[None, :], axis=1)


def reference(screens, interp_weights, footprint, illumination, cm_values, cm_columns, prev_commands, owner_map, dm_gain):
    table, centre_v, centre_u = spectrum_tables(SIDE)
    weights_flat = interp_weights.reshape(LAYERS * FOOT * P_SIZE, P_SIZE)
    groups = SUBS // SUB_DEV

    def sense(pair):
        foot_rows, illum_rows = pair
        picked = jnp.stack([jnp.take(screens[layer], foot_rows[:, layer, :], axis=0) for layer in range(LAYERS)], axis=1)
        picked = picked.reshape(foot_rows.shape[0], LAYERS * FOOT * P_SIZE)
        phase = jnp.dot(picked, weights_flat, preferred_element_type=jnp.float32)
        return spot_slopes(phase, illum_rows, table, centre_v, centre_u)

    parts = lax.map(sense, (footprint.reshape(groups, SUB_DEV, LAYERS, FOOT), illumination.reshape(groups, SUB_DEV, P_SIZE)))
    slopes = jnp.transpose(parts, (1, 0, 2)).reshape(2, SUBS)
    slope_words = slopes.astype(jnp.bfloat16)
    blocks = slope_words.reshape(2, NCB, CBS)
    picked_blocks = jnp.take(blocks, cm_columns, axis=1)
    recon = jnp.einsum("rjics,crjs->ri", cm_values.astype(jnp.float32), picked_blocks.astype(jnp.float32)).reshape(ACT)
    commands = settle(recon, prev_commands, owner_map, dm_gain)
    return slopes, commands
```

```python
import functools
import math

import jax
import jax.numpy as jnp
import numpy as np
from jax import lax
from jax.experimental import pallas as pl
from jax.experimental.pallas import tpu as pltpu
from jax.sharding import PartitionSpec as P

SIDE = 16
LANES = 128
GROUP = 8
MESH = pl.DeviceIdType.MESH


def transform_table(side):
    index = np.arange(side * side)
    row_ids, col_ids = index // side, index % side
    turns = (row_ids[:, None] * row_ids[None, :] + col_ids[:, None] * col_ids[None, :]) % side
    angle = turns.astype(np.float32) * np.float32(2.0 * math.pi / side)
    cosine, sine = np.cos(angle), np.sin(angle)
    table = np.concatenate(
        [np.concatenate([cosine, -sine], 1), np.concatenate([sine, cosine], 1)], 0
    )
    return jnp.asarray(table.T.astype(jnp.bfloat16))


def gather_table(nonzero, acts, comps):
    width = nonzero * acts * comps
    rows = np.arange(GROUP * width)
    target = (rows // width) * acts + (rows % (acts * comps)) // comps
    table = target[:, None] == np.arange(GROUP * acts)[None, :]
    return jnp.asarray(table.astype(jnp.bfloat16))


def cos_sin(x):
    turns = jnp.floor(x * np.float32(2.0 / math.pi) + 0.5)
    r = x - turns * np.float32(1.5703125)
    r = r - turns * np.float32(4.837512969970703125e-4)
    r = r - turns * np.float32(7.54978995489188216e-8)
    r2 = r * r
    s = np.float32(8.3321608736e-3) + r2 * np.float32(-1.9515295891e-4)
    s = np.float32(-1.6666654611e-1) + r2 * s
    s = r + r * r2 * s
    c = np.float32(-1.388731625493765e-3) + r2 * np.float32(2.443315711809948e-5)
    c = np.float32(4.166664568298827e-2) + r2 * c
    c = (1.0 - 0.5 * r2) + r2 * r2 * c
    quarter = turns.astype(jnp.int32)
    odd = (quarter & 1) == 1
    cosine = jnp.where(odd, s, c)
    sine = jnp.where(odd, c, s)
    cosine = jnp.where(((quarter + 1) & 2) == 2, -cosine, cosine)
    sine = jnp.where((quarter & 2) == 2, -sine, sine)
    return cosine, sine


def one_hot(column, base, width):
    ids = lax.broadcasted_iota(jnp.int32, (column.shape[0], width), 1)
    return jnp.where(column - base == ids, 1.0, 0.0).astype(jnp.bfloat16)


def step_kernel(
    grps,
    tiles,
    screens,
    weights,
    footprint,
    illum,
    cm,
    cols,
    prev,
    owner,
    gain,
    table,
    spread,
    slopes_out,
    commands_out,
    screens_v,
    halo,
    weights_v,
    foot_v,
    illum_v,
    cm_v,
    cols_v,
    prev_v,
    owner_v,
    gain_s,
    table_v,
    spread_v,
    picked,
    words,
    chosen,
    z_v,
    parts,
    sums,
    load_sem,
    screen_sem,
    halo_send,
    halo_recv,
    word_send,
    word_recv,
    part_send,
    part_recv,
    sum_send,
    sum_recv,
):
    layers, blk_dev, pixels = screens.shape
    foot = footprint.shape[1]
    sub_dev = illum.shape[0]
    reach = halo.shape[2]
    mirrors = gain.shape[0]
    per_dev = sub_dev // LANES
    rowblk = cm.shape[0]
    width = cm.shape[1]
    nonzero = cols.shape[0]
    acts = width // (2 * nonzero)
    rows = prev.shape[0]
    devices = grps * tiles
    my_grp = lax.axis_index("grp")
    my_tile = lax.axis_index("tile")
    me = my_grp * tiles + my_tile

    def place(device):
        return (device // tiles, device % tiles)

    barrier = pltpu.get_barrier_semaphore()

    def greet(offset, carry):
        pl.semaphore_signal(
            barrier,
            inc=1,
            device_id=place(lax.rem(me + offset, devices)),
            device_id_type=MESH,
        )
        return carry

    lax.fori_loop(1, devices, greet, 0)

    loads = {}
    for number, (name, src, dst) in enumerate(
        [
            ("foot", footprint, foot_v),
            ("weights", weights, weights_v),
            ("cols", cols, cols_v),
            ("gain", gain, gain_s),
            ("prev", prev, prev_v),
            ("owner", owner, owner_v),
            ("illum", illum, illum_v),
            ("table", table, table_v),
            ("spread", spread, spread_v),
            ("cm", cm, cm_v),
        ]
    ):
        loads[name] = pltpu.make_async_copy(src, dst, load_sem.at[number])
    screen_loads = [
        pltpu.make_async_copy(screens.at[layer], screens_v.at[layer], screen_sem.at[layer])
        for layer in range(layers)
    ]
    loads["foot"].start()
    for load in screen_loads:
        load.start()
    for name in loads:
        if name != "foot":
            loads[name].start()

    pl.semaphore_wait(barrier, devices - 1)

    last = lax.rem(me + devices - 1, devices)
    following = lax.rem(me + 1, devices)
    halo_copies = []
    for layer in range(layers):
        for side, (first, target) in enumerate([(blk_dev - reach, following), (0, last)]):
            copy = pltpu.make_async_remote_copy(
                src_ref=screens.at[layer, pl.ds(first, reach)],
                dst_ref=halo.at[layer, side],
                send_sem=halo_send.at[layer, side],
                recv_sem=halo_recv.at[layer, side],
                device_id=place(target),
                device_id_type=MESH,
            )
            copy.start()
            halo_copies.append(copy)

    loads["foot"].wait()
    columns = []
    for layer in range(layers):
        local = foot_v[layer] - (me * blk_dev - reach)
        local = jnp.where(local < 0, local + blk_dev * devices, local)
        local = jnp.where(local >= blk_dev * devices, local - blk_dev * devices, local)
        flipped = jnp.transpose(local)
        columns.append([flipped[:, k : k + 1] for k in range(foot)])

    for layer in range(layers):
        screen_loads[layer].wait()
        for k in range(foot):
            mine = jnp.dot(
                one_hot(columns[layer][k], reach, blk_dev),
                screens_v[layer],
                preferred_element_type=jnp.float32,
            )
            picked[layer, k] = mine.astype(jnp.bfloat16)

    loads["cols"].wait()
    lanes = lax.broadcasted_iota(jnp.int32, (rowblk, width), 1)
    col_ids = jnp.transpose(cols_v[...] - my_grp * (tiles * per_dev))
    code = jnp.zeros((rowblk, width), jnp.int32)
    for n in range(nonzero):
        code = jnp.where(
            lanes // (acts * 2) == n, jnp.broadcast_to(col_ids[:, n : n + 1], code.shape), code
        )
    code = ((code // per_dev) * 2 + lanes % 2) * per_dev + code % per_dev

    loads["gain"].wait()
    loads["owner"].wait()
    loads["prev"].wait()
    owners = owner_v[...]
    gains = jnp.zeros(owners.shape, jnp.float32)
    for m in range(mirrors):
        gains = jnp.where(owners == m, gain_s[m], gains)

    for name in ("weights", "illum", "table", "spread", "cm"):
        loads[name].wait()

    phase = jnp.zeros((sub_dev, pixels), jnp.float32)
    for layer in range(layers):
        for side in range(2):
            halo_copies[2 * layer + side].wait_recv()
        around = halo[layer].reshape(2 * reach, pixels)
        for k in range(foot):
            column = columns[layer][k]
            hot = jnp.concatenate(
                [one_hot(column, 0, reach), one_hot(column, reach + blk_dev, reach)], 1
            )
            other = jnp.dot(hot, around, preferred_element_type=jnp.float32)
            both = picked[layer, k] + other.astype(jnp.bfloat16)
            phase += jnp.dot(
                both, weights_v[layer * foot + k], preferred_element_type=jnp.float32
            )

    cosine, sine = cos_sin(phase)
    bright = illum_v[...]
    field = jnp.concatenate([bright * cosine, bright * sine], 1).astype(jnp.bfloat16)
    spectrum = lax.dot_general(
        table_v[...], field, (((1,), (1,)), ((), ())), preferred_element_type=jnp.float32
    )
    real_part, imag_part = spectrum[:pixels], spectrum[pixels:]
    intensity = real_part * real_part + imag_part * imag_part
    freq = lax.broadcasted_iota(jnp.int32, (pixels, sub_dev), 0)
    half = SIDE // 2
    freq_v, freq_u = freq % SIDE, freq // SIDE
    centre_v = (freq_v - jnp.where(freq_v >= half, SIDE, 0)).astype(jnp.float32)
    centre_u = (freq_u - jnp.where(freq_u >= half, SIDE, 0)).astype(jnp.float32)
    total = jnp.sum(intensity, axis=0, keepdims=True)
    slope_x = jnp.sum(intensity * centre_v, axis=0, keepdims=True) / total
    slope_y = jnp.sum(intensity * centre_u, axis=0, keepdims=True) / total
    slopes_out[0:1, :] = slope_x
    slopes_out[1:2, :] = slope_y
    for c, slope in enumerate((slope_x, slope_y)):
        for b in range(per_dev):
            words[my_tile, pl.ds(c * per_dev + b, 1), :] = slope[:, b * LANES : (b + 1) * LANES]

    word_copies = []
    for offset in range(1, tiles):
        copy = pltpu.make_async_remote_copy(
            src_ref=words.at[my_tile],
            dst_ref=words.at[my_tile],
            send_sem=word_send.at[offset],
            recv_sem=word_recv.at[offset],
            device_id=(my_grp, lax.rem(my_tile + offset, tiles)),
            device_id_type=MESH,
        )
        copy.start()
        word_copies.append(copy)
    for copy in word_copies:
        copy.wait_recv()

    height = 2 * per_dev
    for d in range(tiles):
        chosen[d * height : (d + 1) * height, :] = words[d]
    stack = chosen[...].astype(jnp.bfloat16)
    place_ids = lax.broadcasted_iota(jnp.int32, (tiles * height, width), 0)
    z_v[...] = jnp.zeros(z_v.shape, jnp.float32)
    for start in range(0, rowblk, GROUP):
        count = min(GROUP, rowblk - start)
        values = cm_v[start : start + count].reshape(count * width, LANES)
        product = lax.dot_general(
            stack, values, (((1,), (1,)), ((), ())), preferred_element_type=jnp.float32
        )
        for r in range(count):
            wanted = place_ids == code[start + r : start + r + 1, :]
            kept = jnp.where(wanted, product[:, r * width : (r + 1) * width], 0.0)
            z_v[start + r : start + r + 1, :] = jnp.sum(kept, axis=0, keepdims=True)
    out_rows = z_v.shape[0] // GROUP
    wide = jnp.concatenate([z_v[pl.ds(r, out_rows, stride=GROUP), :] for r in range(GROUP)], 1)
    high = wide.astype(jnp.bfloat16)
    rest = wide - high.astype(jnp.float32)
    middle = rest.astype(jnp.bfloat16)
    low = (rest - middle.astype(jnp.float32)).astype(jnp.bfloat16)
    folded = jnp.dot(
        jnp.concatenate([high, middle, low], 0), spread_v[...], preferred_element_type=jnp.float32
    )
    partial = folded[:out_rows] + (folded[out_rows : 2 * out_rows] + folded[2 * out_rows :])

    previous = prev_v[...]
    first_grp = jnp.where(my_grp == 0, 1.0, 0.0).astype(jnp.float32)
    moved = first_grp * previous - gains * partial[:rows]
    lines = []
    for m in range(mirrors):
        lines.append(jnp.sum(jnp.where(owners == m, moved, 0.0), axis=0, keepdims=True))
    for m in range(mirrors):
        lines.append(jnp.sum(jnp.where(owners == m, first_grp, 0.0), axis=0, keepdims=True))
    parts[my_grp] = partial
    for number, line in enumerate(lines):
        sums[me, pl.ds(number, 1), :] = line
    for number in range(len(lines), sums.shape[1]):
        sums[me, pl.ds(number, 1), :] = jnp.zeros((1, LANES), jnp.float32)

    part_copies = []
    for offset in range(1, grps):
        copy = pltpu.make_async_remote_copy(
            src_ref=parts.at[my_grp],
            dst_ref=parts.at[my_grp],
            send_sem=part_send.at[offset],
            recv_sem=part_recv.at[offset],
            device_id=(lax.rem(my_grp + offset, grps), my_tile),
            device_id_type=MESH,
        )
        copy.start()
        part_copies.append(copy)

    def sum_copy(offset):
        return pltpu.make_async_remote_copy(
            src_ref=sums.at[me],
            dst_ref=sums.at[me],
            send_sem=sum_send.at[offset],
            recv_sem=sum_recv.at[offset],
            device_id=place(lax.rem(me + offset, devices)),
            device_id_type=MESH,
        )

    def send_sum(offset, carry):
        sum_copy(offset).start()
        return carry

    def take_sum(offset, carry):
        sum_copy(offset).wait_recv()
        return carry

    def leave_sum(offset, carry):
        sum_copy(offset).wait_send()
        return carry

    lax.fori_loop(1, devices, send_sum, 0)
    for copy in part_copies:
        copy.wait_recv()
    recon = parts[0]
    for g in range(1, grps):
        recon = recon + parts[g]
    updated = previous - gains * recon[:rows]
    lax.fori_loop(1, devices, take_sum, 0)
    everything = jnp.sum(jnp.sum(sums[...], axis=0), axis=1, keepdims=True)
    piston = jnp.zeros(owners.shape, jnp.float32)
    for m in range(mirrors):
        mean = everything[m : m + 1] / everything[mirrors + m : mirrors + m + 1]
        piston = jnp.where(owners == m, mean, piston)
    commands_out[...] = updated - piston

    for copy in halo_copies + word_copies + part_copies:
        copy.wait_send()
    lax.fori_loop(1, devices, leave_sum, 0)


def on_device(
    screens,
    interp_weights,
    footprint,
    illumination,
    cm_values,
    cm_columns,
    prev_commands,
    owner_map,
    dm_gain,
):
    grps, tiles = lax.axis_size("grp"), lax.axis_size("tile")
    devices = grps * tiles
    layers, blk_dev, pixels = screens.shape
    sub_dev = illumination.shape[0]
    foot = footprint.shape[2]
    reach = blk_dev // 4
    rowblk, nonzero, acts, comps, cbs = cm_values.shape
    width = nonzero * acts * comps
    act_dev = prev_commands.shape[0]
    mirrors = dm_gain.shape[0]
    per_dev = sub_dev // cbs
    rows = -(-act_dev // LANES)
    spare = rows * LANES - act_dev
    if spare:
        prev_commands = jnp.pad(prev_commands, (0, spare))
        owner_map = jnp.pad(owner_map, (0, spare), constant_values=-1)
    out_rows = -(-rows // 16) * 16
    sum_rows = -(-2 * mirrors // 8) * 8
    table = transform_table(SIDE)
    spread = gather_table(nonzero, acts, comps)
    operands = (
        screens,
        interp_weights.reshape(layers * foot, pixels, pixels),
        jnp.transpose(footprint, (1, 2, 0)),
        illumination,
        cm_values.reshape(rowblk, width, cbs),
        jnp.transpose(cm_columns),
        prev_commands.reshape(rows, LANES),
        owner_map.reshape(rows, LANES),
        dm_gain,
        table,
        spread,
    )
    scratch = [pltpu.VMEM(screens.shape, screens.dtype)]
    scratch.append(pltpu.VMEM((layers, 2, reach, pixels), screens.dtype))
    for position in (1, 2, 3, 4, 5, 6, 7):
        scratch.append(pltpu.VMEM(operands[position].shape, operands[position].dtype))
    scratch.append(pltpu.SMEM(dm_gain.shape, dm_gain.dtype))
    for position in (9, 10):
        scratch.append(pltpu.VMEM(operands[position].shape, operands[position].dtype))
    scratch += [
        pltpu.VMEM((layers, foot, sub_dev, pixels), jnp.bfloat16),
        pltpu.VMEM((tiles, comps * per_dev, cbs), jnp.float32),
        pltpu.VMEM((tiles * comps * per_dev, cbs), jnp.float32),
        pltpu.VMEM((out_rows * GROUP, width), jnp.float32),
        pltpu.VMEM((grps, out_rows, LANES), jnp.float32),
        pltpu.VMEM((devices, sum_rows, LANES), jnp.float32),
        pltpu.SemaphoreType.DMA((10,)),
        pltpu.SemaphoreType.DMA((layers,)),
        pltpu.SemaphoreType.DMA((layers, 2)),
        pltpu.SemaphoreType.DMA((layers, 2)),
        pltpu.SemaphoreType.DMA((tiles,)),
        pltpu.SemaphoreType.DMA((tiles,)),
        pltpu.SemaphoreType.DMA((grps,)),
        pltpu.SemaphoreType.DMA((grps,)),
        pltpu.SemaphoreType.DMA((devices,)),
        pltpu.SemaphoreType.DMA((devices,)),
    ]
    slopes, commands = pl.pallas_call(
        functools.partial(step_kernel, grps, tiles),
        out_shape=(
            jax.ShapeDtypeStruct((comps, sub_dev), jnp.float32),
            jax.ShapeDtypeStruct((rows, LANES), jnp.float32),
        ),
        in_specs=[pl.BlockSpec(memory_space=pl.ANY)] * len(operands),
        out_specs=(
            pl.BlockSpec(memory_space=pltpu.VMEM),
            pl.BlockSpec(memory_space=pltpu.VMEM),
        ),
        scratch_shapes=scratch,
        compiler_params=pltpu.CompilerParams(
            collective_id=0, has_side_effects=True, vmem_limit_bytes=56 * 1024 * 1024
        ),
    )(*operands)
    return (slopes, commands.reshape(-1)[:act_dev])


def solution(mesh):
    in_specs = (
        P(None, ("grp", "tile"), None),
        P(),
        P(("grp", "tile"), None, None),
        P(("grp", "tile"), None),
        P("tile", "grp", None, None, None),
        P("tile", "grp"),
        P("tile"),
        P("tile"),
        P(),
    )
    out_specs = (P(None, ("grp", "tile")), P("tile"))
    return jax.shard_map(
        on_device, mesh=mesh, in_specs=in_specs, out_specs=out_specs, check_vma=False
    )
```

```python
import functools
import math

import jax
import jax.numpy as jnp
import numpy as np
from jax import lax
from jax.experimental import pallas as pl
from jax.experimental.pallas import tpu as pltpu
from jax.sharding import PartitionSpec as P

SIDE = 16
LANES = 128
SUBLANES = 8
MESH = pl.DeviceIdType.MESH


def transform_table(side):
    index = np.arange(side * side)
    row_ids, col_ids = index // side, index % side
    turns = (row_ids[:, None] * row_ids[None, :] + col_ids[:, None] * col_ids[None, :]) % side
    angle = turns.astype(np.float32) * np.float32(2.0 * math.pi / side)
    cosine, sine = np.cos(angle), np.sin(angle)
    table = np.concatenate(
        [np.concatenate([cosine, -sine], 1), np.concatenate([sine, cosine], 1)], 0
    )
    return jnp.asarray(table.T.astype(jnp.bfloat16))


def cos_sin(x):
    turns = jnp.floor(x * np.float32(2.0 / math.pi) + 0.5)
    r = x - turns * np.float32(1.5703125)
    r = r - turns * np.float32(4.837512969970703125e-4)
    r = r - turns * np.float32(7.54978995489188216e-8)
    r2 = r * r
    s = np.float32(8.3321608736e-3) + r2 * np.float32(-1.9515295891e-4)
    s = np.float32(-1.6666654611e-1) + r2 * s
    s = r + r * r2 * s
    c = np.float32(-1.388731625493765e-3) + r2 * np.float32(2.443315711809948e-5)
    c = np.float32(4.166664568298827e-2) + r2 * c
    c = (1.0 - 0.5 * r2) + r2 * r2 * c
    quarter = turns.astype(jnp.int32)
    odd = (quarter & 1) == 1
    cosine = jnp.where(odd, s, c)
    sine = jnp.where(odd, c, s)
    cosine = jnp.where(((quarter + 1) & 2) == 2, -cosine, cosine)
    sine = jnp.where((quarter & 2) == 2, -sine, sine)
    return cosine, sine


def one_hot(column, base, width):
    ids = lax.broadcasted_iota(jnp.int32, (column.shape[0], width), 1)
    return jnp.where(column - base == ids, 1.0, 0.0).astype(jnp.bfloat16)


def step_kernel(
    grps,
    tiles,
    screens,
    weights,
    footprint,
    illum,
    cm,
    cols,
    prev,
    owner,
    gain,
    table,
    slopes_out,
    commands_out,
    screens_v,
    halo,
    weights_v,
    foot_v,
    illum_v,
    cm_v,
    prev_v,
    owner_v,
    table_v,
    cols_s,
    gain_s,
    picked,
    far_hot,
    wide_cm,
    words,
    parts,
    sums,
    load_sem,
    screen_sem,
    halo_send,
    halo_recv,
    word_send,
    word_recv,
    part_send,
    part_recv,
    sum_send,
    sum_recv,
):
    layers, blk_dev, pixels = screens.shape
    foot = footprint.shape[1]
    sub_dev = illum.shape[0]
    reach = halo.shape[2]
    mirrors = gain.shape[0]
    per_dev = sub_dev // LANES
    rowblk, nonzero, tall = wide_cm.shape[:3]
    acts = tall * SUBLANES // 2
    rows = prev.shape[0]
    per_row = LANES // acts
    devices = grps * tiles
    my_grp = lax.axis_index("grp")
    my_tile = lax.axis_index("tile")
    me = my_grp * tiles + my_tile
    odd = lax.rem(me, 2)

    def place(device):
        return (device // tiles, device % tiles)

    barrier = pltpu.get_barrier_semaphore()

    def greet(offset, carry):
        pl.semaphore_signal(
            barrier,
            inc=1,
            device_id=place(lax.rem(me + offset, devices)),
            device_id_type=MESH,
        )
        return carry

    lax.fori_loop(1, devices, greet, 0)

    loads = {}
    for number, (name, src, dst) in enumerate(
        [
            ("foot", footprint, foot_v),
            ("weights", weights, weights_v),
            ("cols", cols, cols_s),
            ("gain", gain, gain_s),
            ("prev", prev, prev_v),
            ("owner", owner, owner_v),
            ("illum", illum, illum_v),
            ("table", table, table_v),
            ("cm", cm, cm_v),
        ]
    ):
        loads[name] = pltpu.make_async_copy(src, dst, load_sem.at[number])
    screen_loads = [
        pltpu.make_async_copy(screens.at[layer], screens_v.at[layer], screen_sem.at[layer])
        for layer in range(layers)
    ]
    loads["foot"].start()
    for load in screen_loads:
        load.start()
    for name in loads:
        if name != "foot":
            loads[name].start()

    pl.semaphore_wait(barrier, devices - 1)

    edge = blk_dev - reach
    far_copies, near_copies = [], []
    for kind, copies in enumerate((far_copies, near_copies)):
        ahead = odd if kind == 0 else 1 - odd
        target = place(lax.rem(me + devices + 2 * ahead - 1, devices))
        for layer in range(layers):
            copy = pltpu.make_async_remote_copy(
                src_ref=screens.at[layer, pl.ds(pl.multiple_of(edge * ahead, reach), reach)],
                dst_ref=halo.at[layer, kind],
                send_sem=halo_send.at[layer, kind],
                recv_sem=halo_recv.at[layer, kind],
                device_id=target,
                device_id_type=MESH,
            )
            copy.start()
            copies.append(copy)

    loads["foot"].wait()
    columns = []
    for layer in range(layers):
        local = foot_v[layer] - (me * blk_dev - reach)
        local = jnp.where(local < 0, local + blk_dev * devices, local)
        local = jnp.where(local >= blk_dev * devices, local - blk_dev * devices, local)
        flipped = jnp.transpose(local)
        columns.append([flipped[:, k : k + 1] for k in range(foot)])

    for layer in range(layers):
        screen_loads[layer].wait()
        for k in range(foot):
            mine = jnp.dot(
                one_hot(columns[layer][k], reach, blk_dev),
                screens_v[layer],
                preferred_element_type=jnp.float32,
            )
            picked[layer, k] = mine.astype(jnp.bfloat16)

    past = reach + blk_dev
    far_base, near_base = odd * past, (1 - odd) * past
    loads["weights"].wait()
    phase = jnp.zeros((sub_dev, pixels), jnp.float32)
    for layer in range(layers):
        near_copies[layer].wait_recv()
        for k in range(foot):
            column = columns[layer][k]
            near = jnp.dot(
                one_hot(column, near_base, reach),
                halo[layer, 1],
                preferred_element_type=jnp.float32,
            )
            both = picked[layer, k] + near.astype(jnp.bfloat16)
            phase += jnp.dot(
                both, weights_v[layer * foot + k], preferred_element_type=jnp.float32
            )
            far_hot[layer, k] = one_hot(column, far_base, reach)

    loads["cm"].wait()

    def widen(i, carry):
        wide_cm[i] = cm_v[i].astype(jnp.float32).reshape(wide_cm.shape[1:])
        return carry

    lax.fori_loop(0, rowblk, widen, 0)

    for name in ("cols", "gain", "owner", "prev", "illum", "table"):
        loads[name].wait()
    owners = owner_v[...]
    previous = prev_v[...]
    gains = jnp.zeros(owners.shape, jnp.float32)
    for m in range(mirrors):
        gains = jnp.where(owners == m, gain_s[m], gains)
    first_grp = jnp.where(my_grp == 0, 1.0, 0.0).astype(jnp.float32)

    for layer in range(layers):
        far_copies[layer].wait_recv()
        other = jnp.dot(
            far_hot[layer].reshape(foot * sub_dev, reach),
            halo[layer, 0],
            preferred_element_type=jnp.float32,
        ).astype(jnp.bfloat16)
        for k in range(foot):
            phase += jnp.dot(
                other[k * sub_dev : (k + 1) * sub_dev],
                weights_v[layer * foot + k],
                preferred_element_type=jnp.float32,
            )

    cosine, sine = cos_sin(phase)
    bright = illum_v[...]
    field = jnp.concatenate([bright * cosine, bright * sine], 1).astype(jnp.bfloat16)
    spectrum = lax.dot_general(
        table_v[...], field, (((1,), (1,)), ((), ())), preferred_element_type=jnp.float32
    )
    real_part, imag_part = spectrum[:pixels], spectrum[pixels:]
    intensity = real_part * real_part + imag_part * imag_part
    freq = lax.broadcasted_iota(jnp.int32, (pixels, sub_dev), 0)
    half = SIDE // 2
    freq_v, freq_u = freq % SIDE, freq // SIDE
    centre_v = (freq_v - jnp.where(freq_v >= half, SIDE, 0)).astype(jnp.float32)
    centre_u = (freq_u - jnp.where(freq_u >= half, SIDE, 0)).astype(jnp.float32)
    total = jnp.sum(intensity, axis=0, keepdims=True)
    slope_x = jnp.sum(intensity * centre_v, axis=0, keepdims=True) / total
    slope_y = jnp.sum(intensity * centre_u, axis=0, keepdims=True) / total
    tile_row = lax.broadcasted_iota(jnp.int32, (SUBLANES, sub_dev), 0)
    turned = jnp.where(
        tile_row % 2 == 0,
        jnp.broadcast_to(slope_x, tile_row.shape),
        jnp.broadcast_to(slope_y, tile_row.shape),
    )
    turned = turned.astype(jnp.bfloat16).astype(jnp.float32)
    for b in range(per_dev):
        words[my_tile * per_dev + b] = turned[:, b * LANES : (b + 1) * LANES]

    word_copies = []
    mine = pl.ds(my_tile * per_dev, per_dev)
    for offset in range(1, tiles):
        copy = pltpu.make_async_remote_copy(
            src_ref=words.at[mine],
            dst_ref=words.at[mine],
            send_sem=word_send.at[offset],
            recv_sem=word_recv.at[offset],
            device_id=(my_grp, lax.rem(my_tile + offset, tiles)),
            device_id_type=MESH,
        )
        copy.start()
        word_copies.append(copy)
    slopes_out[0:1, :] = slope_x
    slopes_out[1:2, :] = slope_y
    for copy in word_copies:
        copy.wait_recv()

    base_col = my_grp * (tiles * per_dev)
    act_row = (
        lax.broadcasted_iota(jnp.int32, (tall, SUBLANES, LANES), 0) * SUBLANES
        + lax.broadcasted_iota(jnp.int32, (tall, SUBLANES, LANES), 1)
    ) // 2
    lane = lax.broadcasted_iota(jnp.int32, (tall, SUBLANES, LANES), 2)
    for row in range(rows):
        spread = jnp.zeros((tall, SUBLANES, LANES), jnp.float32)
        for r in range(min(per_row, rowblk - row * per_row)):
            i = row * per_row + r
            products = jnp.zeros((tall, SUBLANES, LANES), jnp.float32)
            for n in range(nonzero):
                block = words[jnp.maximum(cols_s[n, i] - base_col, 0)]
                products = products + wide_cm[i, n] * block[None]
            reduced = jnp.sum(products, axis=2, keepdims=True)
            spread = jnp.where(lane == r * acts + act_row, reduced, spread)
        line = jnp.sum(jnp.sum(spread, axis=0), axis=0, keepdims=True)
        parts[my_grp, row : row + 1, :] = line
    partial = parts[my_grp]

    moved = first_grp * previous - gains * partial
    lines = []
    for m in range(mirrors):
        lines.append(jnp.sum(jnp.where(owners == m, moved, 0.0), axis=0, keepdims=True))
    for m in range(mirrors):
        lines.append(jnp.sum(jnp.where(owners == m, first_grp, 0.0), axis=0, keepdims=True))
    sum_row = lax.broadcasted_iota(jnp.int32, sums.shape[1:], 0)
    packed = jnp.zeros(sums.shape[1:], jnp.float32)
    for number, line in enumerate(lines):
        packed = jnp.where(sum_row == number, jnp.broadcast_to(line, packed.shape), packed)
    sums[me] = packed

    part_copies = []
    for offset in range(1, grps):
        copy = pltpu.make_async_remote_copy(
            src_ref=parts.at[my_grp],
            dst_ref=parts.at[my_grp],
            send_sem=part_send.at[offset],
            recv_sem=part_recv.at[offset],
            device_id=(lax.rem(my_grp + offset, grps), my_tile),
            device_id_type=MESH,
        )
        copy.start()
        part_copies.append(copy)

    def send_sum(offset, carry):
        pltpu.make_async_remote_copy(
            src_ref=sums.at[me],
            dst_ref=sums.at[me],
            send_sem=sum_send.at[0],
            recv_sem=sum_recv.at[0],
            device_id=place(lax.rem(me + offset, devices)),
            device_id_type=MESH,
        ).start()
        return carry

    lax.fori_loop(1, devices, send_sum, 0)
    others = sums.at[pl.ds(0, devices - 1)]
    for copy in part_copies:
        copy.wait_recv()
    recon = parts[0]
    for g in range(1, grps):
        recon = recon + parts[g]
    updated = previous - gains * recon
    pltpu.make_async_copy(others, others, sum_recv.at[0]).wait()
    everything = jnp.sum(jnp.sum(sums[...], axis=0), axis=1, keepdims=True)
    piston = jnp.zeros(owners.shape, jnp.float32)
    for m in range(mirrors):
        mean = everything[m : m + 1] / everything[mirrors + m : mirrors + m + 1]
        piston = jnp.where(owners == m, mean, piston)
    commands_out[...] = updated - piston

    for copy in far_copies + near_copies + word_copies + part_copies:
        copy.wait_send()
    pltpu.make_async_copy(others, others, sum_send.at[0]).wait()


def on_device(
    screens,
    interp_weights,
    footprint,
    illumination,
    cm_values,
    cm_columns,
    prev_commands,
    owner_map,
    dm_gain,
):
    grps, tiles = lax.axis_size("grp"), lax.axis_size("tile")
    devices = grps * tiles
    layers, blk_dev, pixels = screens.shape
    sub_dev = illumination.shape[0]
    foot = footprint.shape[2]
    reach = blk_dev // 4
    rowblk, nonzero, acts, comps, cbs = cm_values.shape
    width = nonzero * acts * comps
    act_dev = prev_commands.shape[0]
    mirrors = dm_gain.shape[0]
    per_dev = sub_dev // cbs
    rows = -(-act_dev // LANES)
    spare = rows * LANES - act_dev
    if spare:
        prev_commands = jnp.pad(prev_commands, (0, spare))
        owner_map = jnp.pad(owner_map, (0, spare), constant_values=-1)
    sum_rows = -(-2 * mirrors // SUBLANES) * SUBLANES
    operands = (
        screens,
        interp_weights.reshape(layers * foot, pixels, pixels),
        jnp.transpose(footprint, (1, 2, 0)),
        illumination,
        cm_values.reshape(rowblk, width, cbs),
        jnp.transpose(cm_columns),
        prev_commands.reshape(rows, LANES),
        owner_map.reshape(rows, LANES),
        dm_gain,
        transform_table(SIDE),
    )
    scratch = [pltpu.VMEM(screens.shape, screens.dtype)]
    scratch.append(pltpu.VMEM((layers, 2, reach, pixels), screens.dtype))
    for position in (1, 2, 3, 4, 6, 7, 9):
        scratch.append(pltpu.VMEM(operands[position].shape, operands[position].dtype))
    for position in (5, 8):
        scratch.append(pltpu.SMEM(operands[position].shape, operands[position].dtype))
    scratch += [
        pltpu.VMEM((layers, foot, sub_dev, pixels), jnp.bfloat16),
        pltpu.VMEM((layers, foot, sub_dev, reach), jnp.bfloat16),
        pltpu.VMEM((rowblk, nonzero, acts * comps // SUBLANES, SUBLANES, cbs), jnp.float32),
        pltpu.VMEM((tiles * per_dev, SUBLANES, cbs), jnp.float32),
        pltpu.VMEM((grps, rows, LANES), jnp.float32),
        pltpu.VMEM((devices, sum_rows, LANES), jnp.float32),
        pltpu.SemaphoreType.DMA((9,)),
        pltpu.SemaphoreType.DMA((layers,)),
        pltpu.SemaphoreType.DMA((layers, 2)),
        pltpu.SemaphoreType.DMA((layers, 2)),
        pltpu.SemaphoreType.DMA((tiles,)),
        pltpu.SemaphoreType.DMA((tiles,)),
        pltpu.SemaphoreType.DMA((grps,)),
        pltpu.SemaphoreType.DMA((grps,)),
        pltpu.SemaphoreType.DMA((1,)),
        pltpu.SemaphoreType.DMA((1,)),
    ]
    slopes, commands = pl.pallas_call(
        functools.partial(step_kernel, grps, tiles),
        out_shape=(
            pltpu.VMEM((comps, sub_dev), jnp.float32),
            pltpu.VMEM((rows, LANES), jnp.float32),
        ),
        in_specs=[pl.BlockSpec(memory_space=pl.ANY)] * len(operands),
        out_specs=(
            pl.BlockSpec(memory_space=pltpu.VMEM),
            pl.BlockSpec(memory_space=pltpu.VMEM),
        ),
        scratch_shapes=scratch,
        compiler_params=pltpu.CompilerParams(
            collective_id=0, has_side_effects=True, vmem_limit_bytes=56 * 1024 * 1024
        ),
    )(*operands)
    return (slopes, commands.reshape(-1)[:act_dev])


def solution(mesh):
    in_specs = (
        P(None, ("grp", "tile"), None),
        P(),
        P(("grp", "tile"), None, None),
        P(("grp", "tile"), None),
        P("tile", "grp", None, None, None),
        P("tile", "grp"),
        P("tile"),
        P("tile"),
        P(),
    )
    out_specs = (P(None, ("grp", "tile")), P("tile"))
    return jax.shard_map(
        on_device, mesh=mesh, in_specs=in_specs, out_specs=out_specs, check_vma=False
    )
```

```python
import functools
import math

import jax
import jax.numpy as jnp
import numpy as np
from jax import lax
from jax.experimental import pallas as pl
from jax.experimental.pallas import tpu as pltpu
from jax.sharding import PartitionSpec as P

SIDE = 16
LANES = 128
SUBLANES = 8
MESH = pl.DeviceIdType.MESH


def transform_table(side):
    index = np.arange(side * side)
    row_ids, col_ids = index // side, index % side
    turns = (row_ids[:, None] * row_ids[None, :] + col_ids[:, None] * col_ids[None, :]) % side
    angle = turns.astype(np.float32) * np.float32(2.0 * math.pi / side)
    cosine, sine = np.cos(angle), np.sin(angle)
    table = np.concatenate(
        [np.concatenate([cosine, -sine], 1), np.concatenate([sine, cosine], 1)], 0
    )
    return jnp.asarray(table.T.astype(jnp.bfloat16))


def cos_sin(x):
    turns = jnp.floor(x * np.float32(2.0 / math.pi) + 0.5)
    r = x - turns * np.float32(1.5703125)
    r = r - turns * np.float32(4.837512969970703125e-4)
    r = r - turns * np.float32(7.54978995489188216e-8)
    r2 = r * r
    s = np.float32(8.3321608736e-3) + r2 * np.float32(-1.9515295891e-4)
    s = np.float32(-1.6666654611e-1) + r2 * s
    s = r + r * r2 * s
    c = np.float32(-1.388731625493765e-3) + r2 * np.float32(2.443315711809948e-5)
    c = np.float32(4.166664568298827e-2) + r2 * c
    c = (1.0 - 0.5 * r2) + r2 * r2 * c
    quarter = turns.astype(jnp.int32)
    odd = (quarter & 1) == 1
    cosine = jnp.where(odd, s, c)
    sine = jnp.where(odd, c, s)
    cosine = jnp.where(((quarter + 1) & 2) == 2, -cosine, cosine)
    sine = jnp.where((quarter & 2) == 2, -sine, sine)
    return cosine, sine


def one_hot(column, base, width):
    ids = lax.broadcasted_iota(jnp.int32, (column.shape[0], width), 1)
    return jnp.where(column - base == ids, 1.0, 0.0).astype(jnp.bfloat16)


def ring(start, offset, size):
    place = start + offset
    place = jnp.where(place >= size, place - size, place)
    return jnp.where(place >= size, place - size, place)


def step_kernel(
    grps,
    tiles,
    screens,
    weights,
    footprint,
    illum,
    cm,
    cols,
    prev,
    owner,
    gain,
    table,
    slopes_out,
    commands_out,
    screens_v,
    halo,
    weights_v,
    foot_v,
    illum_v,
    cm_v,
    prev_v,
    owner_v,
    table_v,
    cols_s,
    gain_s,
    picked,
    far_hot,
    wide_cm,
    words,
    blocks,
    parts,
    sums,
    load_sem,
    screen_sem,
    halo_send,
    halo_recv,
    word_send,
    word_recv,
    part_send,
    part_recv,
    sum_send,
    sum_recv,
):
    layers, blk_dev, pixels = screens.shape
    foot = footprint.shape[1]
    sub_dev = illum.shape[0]
    reach = halo.shape[2]
    mirrors = gain.shape[0]
    per_dev = sub_dev // LANES
    rowblk, nonzero, tall = wide_cm.shape[:3]
    acts = tall * SUBLANES // 2
    rows = prev.shape[0]
    per_row = LANES // acts
    devices = grps * tiles
    my_grp = lax.axis_index("grp")
    my_tile = lax.axis_index("tile")
    me = my_grp * tiles + my_tile
    odd = lax.rem(me, 2)
    grp_peers = [ring(my_grp, offset, grps) for offset in range(grps)]
    tile_peers = [ring(my_tile, offset, tiles) for offset in range(tiles)]
    everyone = [(g, t) for t in tile_peers for g in grp_peers][1:]

    barrier = pltpu.get_barrier_semaphore()
    for peer in everyone:
        pl.semaphore_signal(barrier, inc=1, device_id=peer, device_id_type=MESH)

    loads = {}
    for number, (name, src, dst) in enumerate(
        [
            ("foot", footprint, foot_v),
            ("weights", weights, weights_v),
            ("cols", cols, cols_s),
            ("gain", gain, gain_s),
            ("prev", prev, prev_v),
            ("owner", owner, owner_v),
            ("illum", illum, illum_v),
            ("table", table, table_v),
            ("cm", cm, cm_v),
        ]
    ):
        loads[name] = pltpu.make_async_copy(src, dst, load_sem.at[number])
    screen_loads = [
        pltpu.make_async_copy(screens.at[layer], screens_v.at[layer], screen_sem.at[layer])
        for layer in range(layers)
    ]
    loads["foot"].start()
    for load in screen_loads:
        load.start()
    for name in loads:
        if name != "foot":
            loads[name].start()

    pl.semaphore_wait(barrier, devices - 1)

    edge = blk_dev - reach
    far_copies, near_copies = [], []
    for kind, copies in enumerate((far_copies, near_copies)):
        ahead = odd if kind == 0 else 1 - odd
        tile = my_tile + 2 * ahead - 1
        turn = jnp.where(tile >= tiles, 1, jnp.where(tile < 0, -1, 0))
        target = (ring(my_grp + turn, grps, grps), tile - turn * tiles)
        for layer in range(layers):
            copy = pltpu.make_async_remote_copy(
                src_ref=screens.at[layer, pl.ds(pl.multiple_of(edge * ahead, reach), reach)],
                dst_ref=halo.at[layer, kind],
                send_sem=halo_send.at[layer, kind],
                recv_sem=halo_recv.at[layer, kind],
                device_id=target,
                device_id_type=MESH,
            )
            copy.start()
            copies.append(copy)

    loads["foot"].wait()
    columns = []
    for layer in range(layers):
        local = foot_v[layer] - (me * blk_dev - reach)
        local = jnp.where(local < 0, local + blk_dev * devices, local)
        local = jnp.where(local >= blk_dev * devices, local - blk_dev * devices, local)
        flipped = jnp.transpose(local)
        columns.append([flipped[:, k : k + 1] for k in range(foot)])

    for layer in range(layers):
        screen_loads[layer].wait()
        for k in range(foot):
            mine = jnp.dot(
                one_hot(columns[layer][k], reach, blk_dev),
                screens_v[layer],
                preferred_element_type=jnp.float32,
            )
            picked[layer, k] = mine.astype(jnp.bfloat16)

    past = reach + blk_dev
    far_base, near_base = odd * past, (1 - odd) * past
    loads["weights"].wait()
    phase = jnp.zeros((sub_dev, pixels), jnp.float32)
    for layer in range(layers):
        near_copies[layer].wait_recv()
        for k in range(foot):
            column = columns[layer][k]
            near = jnp.dot(
                one_hot(column, near_base, reach),
                halo[layer, 1],
                preferred_element_type=jnp.float32,
            )
            both = picked[layer, k] + near.astype(jnp.bfloat16)
            phase += jnp.dot(
                both, weights_v[layer * foot + k], preferred_element_type=jnp.float32
            )
            far_hot[layer, k] = one_hot(column, far_base, reach)

    loads["cm"].wait()

    def widen(i, carry):
        wide_cm[i] = cm_v[i].astype(jnp.float32).reshape(wide_cm.shape[1:])
        return carry

    lax.fori_loop(0, rowblk, widen, 0)

    for name in ("cols", "gain", "owner", "prev", "illum", "table"):
        loads[name].wait()
    owners = owner_v[...]
    previous = prev_v[...]
    gains = jnp.zeros(owners.shape, jnp.float32)
    for m in range(mirrors):
        gains = jnp.where(owners == m, gain_s[m], gains)
    first_grp = jnp.where(my_grp == 0, 1.0, 0.0).astype(jnp.float32)

    for layer in range(layers):
        far_copies[layer].wait_recv()
        other = jnp.dot(
            far_hot[layer].reshape(foot * sub_dev, reach),
            halo[layer, 0],
            preferred_element_type=jnp.float32,
        ).astype(jnp.bfloat16)
        for k in range(foot):
            phase += jnp.dot(
                other[k * sub_dev : (k + 1) * sub_dev],
                weights_v[layer * foot + k],
                preferred_element_type=jnp.float32,
            )

    cosine, sine = cos_sin(phase)
    bright = illum_v[...]
    field = jnp.concatenate([bright * cosine, bright * sine], 1).astype(jnp.bfloat16)
    spectrum = lax.dot_general(
        table_v[...], field, (((1,), (1,)), ((), ())), preferred_element_type=jnp.float32
    )
    real_part, imag_part = spectrum[:pixels], spectrum[pixels:]
    intensity = real_part * real_part + imag_part * imag_part
    freq = lax.broadcasted_iota(jnp.int32, (pixels, sub_dev), 0)
    half = SIDE // 2
    freq_v, freq_u = freq % SIDE, freq // SIDE
    centre_v = (freq_v - jnp.where(freq_v >= half, SIDE, 0)).astype(jnp.float32)
    centre_u = (freq_u - jnp.where(freq_u >= half, SIDE, 0)).astype(jnp.float32)
    total = jnp.sum(intensity, axis=0, keepdims=True)
    slope_x = jnp.sum(intensity * centre_v, axis=0, keepdims=True) / total
    slope_y = jnp.sum(intensity * centre_u, axis=0, keepdims=True) / total
    for c, slope in enumerate((slope_x, slope_y)):
        for b in range(per_dev):
            word = slope[:, b * LANES : (b + 1) * LANES].astype(jnp.bfloat16)
            words[my_tile, pl.ds(c * per_dev + b, 1), :] = word.astype(jnp.float32)

    word_copies = []
    for offset in range(1, tiles):
        copy = pltpu.make_async_remote_copy(
            src_ref=words.at[my_tile],
            dst_ref=words.at[my_tile],
            send_sem=word_send.at[offset],
            recv_sem=word_recv.at[offset],
            device_id=(my_grp, tile_peers[offset]),
            device_id_type=MESH,
        )
        copy.start()
        word_copies.append(copy)
    slopes_out[0:1, :] = slope_x
    slopes_out[1:2, :] = slope_y
    for copy in word_copies:
        copy.wait_recv()

    x_row = lax.broadcasted_iota(jnp.int32, (SUBLANES, LANES), 0) % 2 == 0
    for d in range(tiles):
        for b in range(per_dev):
            blocks[d * per_dev + b] = jnp.where(
                x_row,
                jnp.broadcast_to(words[d, b : b + 1, :], x_row.shape),
                jnp.broadcast_to(words[d, per_dev + b : per_dev + b + 1, :], x_row.shape),
            )

    base_col = my_grp * (tiles * per_dev)
    act_row = (
        lax.broadcasted_iota(jnp.int32, (tall, SUBLANES, LANES), 0) * SUBLANES
        + lax.broadcasted_iota(jnp.int32, (tall, SUBLANES, LANES), 1)
    ) // 2
    lane = lax.broadcasted_iota(jnp.int32, (tall, SUBLANES, LANES), 2)
    for row in range(rows):
        spread = jnp.zeros((tall, SUBLANES, LANES), jnp.float32)
        for r in range(min(per_row, rowblk - row * per_row)):
            i = row * per_row + r
            products = jnp.zeros((tall, SUBLANES, LANES), jnp.float32)
            for n in range(nonzero):
                block = blocks[jnp.maximum(cols_s[n, i] - base_col, 0)]
                products = products + wide_cm[i, n] * block[None]
            reduced = jnp.sum(products, axis=2, keepdims=True)
            spread = jnp.where(lane == r * acts + act_row, reduced, spread)
        line = jnp.sum(jnp.sum(spread, axis=0), axis=0, keepdims=True)
        parts[my_grp, row : row + 1, :] = line
    partial = parts[my_grp]

    moved = first_grp * previous - gains * partial
    sum_lane = lax.broadcasted_iota(jnp.int32, sums.shape[1:], 1)
    packed = jnp.zeros(sums.shape[1:], jnp.float32)
    for m in range(mirrors):
        amount = jnp.sum(jnp.where(owners == m, moved, 0.0), axis=0, keepdims=True)
        number = jnp.sum(jnp.where(owners == m, first_grp, 0.0), axis=0, keepdims=True)
        packed = jnp.where(sum_lane == m, jnp.sum(amount, axis=1, keepdims=True), packed)
        packed = jnp.where(
            sum_lane == mirrors + m, jnp.sum(number, axis=1, keepdims=True), packed
        )
    sums[me] = packed

    part_copies = []
    for offset in range(1, grps):
        copy = pltpu.make_async_remote_copy(
            src_ref=parts.at[my_grp],
            dst_ref=parts.at[my_grp],
            send_sem=part_send.at[offset],
            recv_sem=part_recv.at[offset],
            device_id=(grp_peers[offset], my_tile),
            device_id_type=MESH,
        )
        copy.start()
        part_copies.append(copy)

    for peer in everyone:
        pltpu.make_async_remote_copy(
            src_ref=sums.at[me],
            dst_ref=sums.at[me],
            send_sem=sum_send.at[0],
            recv_sem=sum_recv.at[0],
            device_id=peer,
            device_id_type=MESH,
        ).start()
    others = sums.at[pl.ds(0, devices - 1)]
    for copy in part_copies:
        copy.wait_recv()
    recon = parts[0]
    for g in range(1, grps):
        recon = recon + parts[g]
    updated = previous - gains * recon
    pltpu.make_async_copy(others, others, sum_recv.at[0]).wait()
    everything = jnp.sum(sums[...], axis=0)
    piston = jnp.zeros(owners.shape, jnp.float32)
    for m in range(mirrors):
        mean = everything[:, m : m + 1] / everything[:, mirrors + m : mirrors + m + 1]
        piston = jnp.where(owners == m, mean, piston)
    commands_out[...] = updated - piston

    for copy in far_copies + near_copies + word_copies + part_copies:
        copy.wait_send()
    pltpu.make_async_copy(others, others, sum_send.at[0]).wait()


def write_out(slopes, commands, slopes_out, commands_out, sem):
    first = pltpu.make_async_copy(slopes, slopes_out, sem.at[0])
    second = pltpu.make_async_copy(commands, commands_out, sem.at[1])
    first.start()
    second.start()
    first.wait()
    second.wait()


def on_device(
    screens,
    interp_weights,
    footprint,
    illumination,
    cm_values,
    cm_columns,
    prev_commands,
    owner_map,
    dm_gain,
):
    grps, tiles = lax.axis_size("grp"), lax.axis_size("tile")
    devices = grps * tiles
    layers, blk_dev, pixels = screens.shape
    sub_dev = illumination.shape[0]
    foot = footprint.shape[2]
    reach = blk_dev // 4
    rowblk, nonzero, acts, comps, cbs = cm_values.shape
    width = nonzero * acts * comps
    act_dev = prev_commands.shape[0]
    mirrors = dm_gain.shape[0]
    per_dev = sub_dev // cbs
    rows = -(-act_dev // LANES)
    spare = rows * LANES - act_dev
    if spare:
        prev_commands = jnp.pad(prev_commands, (0, spare))
        owner_map = jnp.pad(owner_map, (0, spare), constant_values=-1)
    operands = (
        screens,
        interp_weights.reshape(layers * foot, pixels, pixels),
        jnp.transpose(footprint, (1, 2, 0)),
        illumination,
        cm_values.reshape(rowblk, width, cbs),
        jnp.transpose(cm_columns),
        prev_commands.reshape(rows, LANES),
        owner_map.reshape(rows, LANES),
        dm_gain,
        transform_table(SIDE),
    )
    scratch = [pltpu.VMEM(screens.shape, screens.dtype)]
    scratch.append(pltpu.VMEM((layers, 2, reach, pixels), screens.dtype))
    for position in (1, 2, 3, 4, 6, 7, 9):
        scratch.append(pltpu.VMEM(operands[position].shape, operands[position].dtype))
    for position in (5, 8):
        scratch.append(pltpu.SMEM(operands[position].shape, operands[position].dtype))
    scratch += [
        pltpu.VMEM((layers, foot, sub_dev, pixels), jnp.bfloat16),
        pltpu.VMEM((layers, foot, sub_dev, reach), jnp.bfloat16),
        pltpu.VMEM((rowblk, nonzero, acts * comps // SUBLANES, SUBLANES, cbs), jnp.float32),
        pltpu.VMEM((tiles, comps * per_dev, cbs), jnp.float32),
        pltpu.VMEM((tiles * per_dev, SUBLANES, cbs), jnp.float32),
        pltpu.VMEM((grps, rows, LANES), jnp.float32),
        pltpu.VMEM((devices, 1, LANES), jnp.float32),
        pltpu.SemaphoreType.DMA((9,)),
        pltpu.SemaphoreType.DMA((layers,)),
        pltpu.SemaphoreType.DMA((layers, 2)),
        pltpu.SemaphoreType.DMA((layers, 2)),
        pltpu.SemaphoreType.DMA((tiles,)),
        pltpu.SemaphoreType.DMA((tiles,)),
        pltpu.SemaphoreType.DMA((grps,)),
        pltpu.SemaphoreType.DMA((grps,)),
        pltpu.SemaphoreType.DMA((1,)),
        pltpu.SemaphoreType.DMA((1,)),
    ]
    slopes, commands = pl.pallas_call(
        functools.partial(step_kernel, grps, tiles),
        out_shape=(
            pltpu.VMEM((comps, sub_dev), jnp.float32),
            pltpu.VMEM((rows, LANES), jnp.float32),
        ),
        in_specs=[pl.BlockSpec(memory_space=pl.ANY)] * len(operands),
        out_specs=(
            pl.BlockSpec(memory_space=pltpu.VMEM),
            pl.BlockSpec(memory_space=pltpu.VMEM),
        ),
        scratch_shapes=scratch,
        compiler_params=pltpu.CompilerParams(
            collective_id=0, has_side_effects=True, vmem_limit_bytes=56 * 1024 * 1024
        ),
    )(*operands)
    slopes, commands = pl.pallas_call(
        write_out,
        out_shape=(
            jax.ShapeDtypeStruct(slopes.shape, slopes.dtype),
            jax.ShapeDtypeStruct(commands.shape, commands.dtype),
        ),
        in_specs=[pl.BlockSpec(memory_space=pltpu.VMEM)] * 2,
        out_specs=(pl.BlockSpec(memory_space=pltpu.HBM), pl.BlockSpec(memory_space=pltpu.HBM)),
        scratch_shapes=[pltpu.SemaphoreType.DMA((2,))],
    )(slopes, commands)
    return (slopes, commands.reshape(-1)[:act_dev])


def solution(mesh):
    in_specs = (
        P(None, ("grp", "tile"), None),
        P(),
        P(("grp", "tile"), None, None),
        P(("grp", "tile"), None),
        P("tile", "grp", None, None, None),
        P("tile", "grp"),
        P("tile"),
        P("tile"),
        P(),
    )
    out_specs = (P(None, ("grp", "tile")), P("tile"))
    return jax.shard_map(
        on_device, mesh=mesh, in_specs=in_specs, out_specs=out_specs, check_vma=False
    )
```

```python
import functools
import math

import jax
import jax.numpy as jnp
import numpy as np
from jax import lax
from jax.experimental import pallas as pl
from jax.experimental.pallas import tpu as pltpu
from jax.sharding import PartitionSpec as P

SIDE = 16
LANES = 128
SUBLANES = 8
MESH = pl.DeviceIdType.MESH


def transform_table(side):
    index = np.arange(side * side)
    row_ids, col_ids = index // side, index % side
    turns = (row_ids[:, None] * row_ids[None, :] + col_ids[:, None] * col_ids[None, :]) % side
    angle = turns.astype(np.float32) * np.float32(2.0 * math.pi / side)
    cosine, sine = np.cos(angle), np.sin(angle)
    table = np.concatenate(
        [np.concatenate([cosine, -sine], 1), np.concatenate([sine, cosine], 1)], 0
    )
    return jnp.asarray(table.T.astype(jnp.bfloat16))


def cos_sin(x):
    turns = jnp.floor(x * np.float32(2.0 / math.pi) + 0.5)
    r = x - turns * np.float32(1.5703125)
    r = r - turns * np.float32(4.837512969970703125e-4)
    r = r - turns * np.float32(7.54978995489188216e-8)
    r2 = r * r
    s = np.float32(8.3321608736e-3) + r2 * np.float32(-1.9515295891e-4)
    s = np.float32(-1.6666654611e-1) + r2 * s
    s = r + r * r2 * s
    c = np.float32(-1.388731625493765e-3) + r2 * np.float32(2.443315711809948e-5)
    c = np.float32(4.166664568298827e-2) + r2 * c
    c = (1.0 - 0.5 * r2) + r2 * r2 * c
    quarter = turns.astype(jnp.int32)
    odd = (quarter & 1) == 1
    cosine = jnp.where(odd, s, c)
    sine = jnp.where(odd, c, s)
    cosine = jnp.where(((quarter + 1) & 2) == 2, -cosine, cosine)
    sine = jnp.where((quarter & 2) == 2, -sine, sine)
    return cosine, sine


def one_hot(ids, base, width):
    lane = lax.broadcasted_iota(jnp.int32, ids.shape, 1) + base
    hot = [jnp.where(ids == lane + first, 1.0, 0.0) for first in range(0, width, LANES)]
    return jnp.concatenate(hot, 1).astype(jnp.bfloat16)


def ring(start, offset, size):
    place = start + offset
    place = jnp.where(place >= size, place - size, place)
    return jnp.where(place >= size, place - size, place)


def step_kernel(
    grps,
    tiles,
    screens,
    weights,
    footprint,
    illum,
    cm,
    cols,
    prev,
    owner,
    gain,
    table,
    slopes_out,
    commands_out,
    screens_v,
    halo,
    weights_v,
    foot_v,
    illum_v,
    cm_v,
    prev_v,
    owner_v,
    table_v,
    cols_s,
    gain_s,
    ids_v,
    picked,
    far_hot,
    wide_cm,
    words,
    blocks,
    parts,
    sums,
    load_sem,
    screen_sem,
    halo_send,
    halo_recv,
    word_send,
    word_recv,
    part_send,
    part_recv,
    sum_send,
    sum_recv,
):
    layers, blk_dev, pixels = screens.shape
    foot = footprint.shape[1]
    sub_dev = illum.shape[0]
    reach = halo.shape[2]
    mirrors = gain.shape[0]
    per_dev = sub_dev // LANES
    rowblk, nonzero, tall = wide_cm.shape[:3]
    acts = tall * SUBLANES // 2
    rows = prev.shape[0]
    per_row = LANES // acts
    devices = grps * tiles
    my_grp = lax.axis_index("grp")
    my_tile = lax.axis_index("tile")
    me = my_grp * tiles + my_tile
    odd = lax.rem(me, 2)
    grp_peers = [ring(my_grp, offset, grps) for offset in range(grps)]
    tile_peers = [ring(my_tile, offset, tiles) for offset in range(tiles)]
    everyone = [(g, t) for t in tile_peers for g in grp_peers][1:]

    barrier = pltpu.get_barrier_semaphore()
    for peer in everyone:
        pl.semaphore_signal(barrier, inc=1, device_id=peer, device_id_type=MESH)

    loads = {}
    for number, (name, src, dst) in enumerate(
        [
            ("foot", footprint, foot_v),
            ("weights", weights, weights_v),
            ("cols", cols, cols_s),
            ("gain", gain, gain_s),
            ("prev", prev, prev_v),
            ("owner", owner, owner_v),
            ("illum", illum, illum_v),
            ("table", table, table_v),
            ("cm", cm, cm_v),
        ]
    ):
        loads[name] = pltpu.make_async_copy(src, dst, load_sem.at[number])
    screen_loads = [
        pltpu.make_async_copy(screens.at[layer], screens_v.at[layer], screen_sem.at[layer])
        for layer in range(layers)
    ]
    loads["foot"].start()
    for load in screen_loads:
        load.start()
    for name in loads:
        if name != "foot":
            loads[name].start()

    pl.semaphore_wait(barrier, devices - 1)

    edge = blk_dev - reach
    far_copies, near_copies = [], []
    for kind, copies in enumerate((far_copies, near_copies)):
        ahead = odd if kind == 0 else 1 - odd
        tile = my_tile + 2 * ahead - 1
        turn = jnp.where(tile >= tiles, 1, jnp.where(tile < 0, -1, 0))
        target = (ring(my_grp + turn, grps, grps), tile - turn * tiles)
        for layer in range(layers):
            copy = pltpu.make_async_remote_copy(
                src_ref=screens.at[layer, pl.ds(pl.multiple_of(edge * ahead, reach), reach)],
                dst_ref=halo.at[layer, kind],
                send_sem=halo_send.at[layer, kind],
                recv_sem=halo_recv.at[layer, kind],
                device_id=target,
                device_id_type=MESH,
            )
            copy.start()
            copies.append(copy)

    loads["foot"].wait()
    for layer in range(layers):
        local = foot_v[layer] - (me * blk_dev - reach)
        local = jnp.where(local < 0, local + blk_dev * devices, local)
        local = jnp.where(local >= blk_dev * devices, local - blk_dev * devices, local)
        flipped = jnp.transpose(local)
        for k in range(foot):
            ids_v[layer, k * sub_dev : (k + 1) * sub_dev, :] = jnp.broadcast_to(
                flipped[:, k : k + 1], (sub_dev, LANES)
            )

    def pick(layer, base, blocks_ref):
        hot = one_hot(ids_v[layer], base, blocks_ref.shape[0])
        return jnp.dot(hot, blocks_ref[...], preferred_element_type=jnp.float32).astype(
            jnp.bfloat16
        )

    def weigh(layer, found):
        side_by_side = jnp.concatenate(
            [found[k * sub_dev : (k + 1) * sub_dev] for k in range(foot)], 1
        )
        own_weights = weights_v[layer * foot : (layer + 1) * foot]
        return jnp.dot(
            side_by_side,
            own_weights.reshape(foot * pixels, pixels),
            preferred_element_type=jnp.float32,
        )

    for layer in range(layers):
        screen_loads[layer].wait()
        picked[layer] = pick(layer, reach, screens_v.at[layer, pl.ds(0, reach)])
        for first in range(reach, blk_dev, reach):
            picked[layer] += pick(layer, reach + first, screens_v.at[layer, pl.ds(first, reach)])

    past = reach + blk_dev
    far_base, near_base = odd * past, (1 - odd) * past
    loads["weights"].wait()
    phase = jnp.zeros((sub_dev, pixels), jnp.float32)
    for layer in range(layers):
        near_copies[layer].wait_recv()
        phase += weigh(layer, picked[layer] + pick(layer, near_base, halo.at[layer, 1]))
    for layer in range(layers):
        far_hot[layer] = one_hot(ids_v[layer], far_base, reach)

    for name in ("cols", "gain", "owner", "prev", "illum", "table"):
        loads[name].wait()
    owners = owner_v[...]
    previous = prev_v[...]
    gains = jnp.zeros(owners.shape, jnp.float32)
    for m in range(mirrors):
        gains = jnp.where(owners == m, gain_s[m], gains)
    first_grp = jnp.where(my_grp == 0, 1.0, 0.0).astype(jnp.float32)

    for layer in range(layers):
        far_copies[layer].wait_recv()
        other = jnp.dot(far_hot[layer], halo[layer, 0], preferred_element_type=jnp.float32)
        phase += weigh(layer, other.astype(jnp.bfloat16))

    cosine, sine = cos_sin(phase)
    bright = illum_v[...]
    field = jnp.concatenate([bright * cosine, bright * sine], 1).astype(jnp.bfloat16)
    spectrum = lax.dot_general(
        table_v[...], field, (((1,), (1,)), ((), ())), preferred_element_type=jnp.float32
    )
    real_part, imag_part = spectrum[:pixels], spectrum[pixels:]
    intensity = real_part * real_part + imag_part * imag_part
    half = SIDE // 2
    wave = lax.broadcasted_iota(jnp.int32, (half, sub_dev), 0).astype(jnp.float32)
    low_v = jnp.zeros((half, sub_dev), jnp.float32)
    high_v = jnp.zeros((half, sub_dev), jnp.float32)
    moment_u = jnp.zeros((half, sub_dev), jnp.float32)
    for u in range(SIDE):
        low = intensity[u * SIDE : u * SIDE + half]
        high = intensity[u * SIDE + half : (u + 1) * SIDE]
        low_v, high_v = low_v + low, high_v + high
        centre_u = float(u - SIDE * (u >= half))
        moment_u = moment_u + centre_u * (low + high)
    moment_v = wave * low_v + (wave - half) * high_v
    total = jnp.sum(low_v + high_v, axis=0, keepdims=True)
    slope_x = jnp.sum(moment_v, axis=0, keepdims=True) / total
    slope_y = jnp.sum(moment_u, axis=0, keepdims=True) / total
    for c, slope in enumerate((slope_x, slope_y)):
        for b in range(per_dev):
            word = slope[:, b * LANES : (b + 1) * LANES].astype(jnp.bfloat16)
            words[my_tile, pl.ds(c * per_dev + b, 1), :] = word.astype(jnp.float32)

    word_copies = []
    for offset in range(1, tiles):
        copy = pltpu.make_async_remote_copy(
            src_ref=words.at[my_tile],
            dst_ref=words.at[my_tile],
            send_sem=word_send.at[offset],
            recv_sem=word_recv.at[offset],
            device_id=(my_grp, tile_peers[offset]),
            device_id_type=MESH,
        )
        copy.start()
        word_copies.append(copy)
    slopes_out[0:1, :] = slope_x
    slopes_out[1:2, :] = slope_y
    loads["cm"].wait()
    for i in range(rowblk):
        wide_cm[i] = cm_v[i].astype(jnp.float32).reshape(wide_cm.shape[1:])
    for copy in word_copies:
        copy.wait_recv()

    x_row = lax.broadcasted_iota(jnp.int32, (SUBLANES, LANES), 0) % 2 == 0
    for d in range(tiles):
        for b in range(per_dev):
            blocks[d * per_dev + b] = jnp.where(
                x_row,
                jnp.broadcast_to(words[d, b : b + 1, :], x_row.shape),
                jnp.broadcast_to(words[d, per_dev + b : per_dev + b + 1, :], x_row.shape),
            )

    base_col = my_grp * (tiles * per_dev)
    act_row = (
        lax.broadcasted_iota(jnp.int32, (tall, SUBLANES, LANES), 0) * SUBLANES
        + lax.broadcasted_iota(jnp.int32, (tall, SUBLANES, LANES), 1)
    ) // 2
    lane = lax.broadcasted_iota(jnp.int32, (tall, SUBLANES, LANES), 2)
    for row in range(rows):
        spread = jnp.zeros((tall, SUBLANES, LANES), jnp.float32)
        for r in range(min(per_row, rowblk - row * per_row)):
            i = row * per_row + r
            products = jnp.zeros((tall, SUBLANES, LANES), jnp.float32)
            for n in range(nonzero):
                block = blocks[jnp.maximum(cols_s[n, i] - base_col, 0)]
                products = products + wide_cm[i, n] * block[None]
            reduced = jnp.sum(products, axis=2, keepdims=True)
            spread = jnp.where(lane == r * acts + act_row, reduced, spread)
        line = jnp.sum(jnp.sum(spread, axis=0), axis=0, keepdims=True)
        parts[my_grp, row : row + 1, :] = line
    partial = parts[my_grp]

    moved = first_grp * previous - gains * partial
    sum_lane = lax.broadcasted_iota(jnp.int32, sums.shape[1:], 1)
    packed = jnp.zeros(sums.shape[1:], jnp.float32)
    for m in range(mirrors):
        amount = jnp.sum(jnp.where(owners == m, moved, 0.0), axis=0, keepdims=True)
        number = jnp.sum(jnp.where(owners == m, first_grp, 0.0), axis=0, keepdims=True)
        packed = jnp.where(sum_lane == m, jnp.sum(amount, axis=1, keepdims=True), packed)
        packed = jnp.where(
            sum_lane == mirrors + m, jnp.sum(number, axis=1, keepdims=True), packed
        )
    sums[me] = packed

    part_copies = []
    for offset in range(1, grps):
        copy = pltpu.make_async_remote_copy(
            src_ref=parts.at[my_grp],
            dst_ref=parts.at[my_grp],
            send_sem=part_send.at[offset],
            recv_sem=part_recv.at[offset],
            device_id=(grp_peers[offset], my_tile),
            device_id_type=MESH,
        )
        copy.start()
        part_copies.append(copy)

    for peer in everyone:
        pltpu.make_async_remote_copy(
            src_ref=sums.at[me],
            dst_ref=sums.at[me],
            send_sem=sum_send.at[0],
            recv_sem=sum_recv.at[0],
            device_id=peer,
            device_id_type=MESH,
        ).start()
    others = sums.at[pl.ds(0, devices - 1)]
    for copy in part_copies:
        copy.wait_recv()
    recon = parts[0]
    for g in range(1, grps):
        recon = recon + parts[g]
    updated = previous - gains * recon
    pltpu.make_async_copy(others, others, sum_recv.at[0]).wait()
    everything = jnp.sum(sums[...], axis=0)
    piston = jnp.zeros(owners.shape, jnp.float32)
    for m in range(mirrors):
        mean = everything[:, m : m + 1] / everything[:, mirrors + m : mirrors + m + 1]
        piston = jnp.where(owners == m, mean, piston)
    commands_out[...] = updated - piston

    for copy in far_copies + near_copies + word_copies + part_copies:
        copy.wait_send()
    pltpu.make_async_copy(others, others, sum_send.at[0]).wait()


def on_device(
    screens,
    interp_weights,
    footprint,
    illumination,
    cm_values,
    cm_columns,
    prev_commands,
    owner_map,
    dm_gain,
):
    grps, tiles = lax.axis_size("grp"), lax.axis_size("tile")
    devices = grps * tiles
    layers, blk_dev, pixels = screens.shape
    sub_dev = illumination.shape[0]
    foot = footprint.shape[2]
    reach = blk_dev // 4
    rowblk, nonzero, acts, comps, cbs = cm_values.shape
    width = nonzero * acts * comps
    act_dev = prev_commands.shape[0]
    mirrors = dm_gain.shape[0]
    per_dev = sub_dev // cbs
    rows = -(-act_dev // LANES)
    spare = rows * LANES - act_dev
    if spare:
        prev_commands = jnp.pad(prev_commands, (0, spare))
        owner_map = jnp.pad(owner_map, (0, spare), constant_values=-1)
    operands = (
        screens,
        interp_weights.reshape(layers * foot, pixels, pixels),
        jnp.transpose(footprint, (1, 2, 0)),
        illumination,
        cm_values.reshape(rowblk, width, cbs),
        jnp.transpose(cm_columns),
        prev_commands.reshape(rows, LANES),
        owner_map.reshape(rows, LANES),
        dm_gain,
        transform_table(SIDE),
    )
    scratch = [pltpu.VMEM(screens.shape, screens.dtype)]
    scratch.append(pltpu.VMEM((layers, 2, reach, pixels), screens.dtype))
    for position in (1, 2, 3, 4, 6, 7, 9):
        scratch.append(pltpu.VMEM(operands[position].shape, operands[position].dtype))
    for position in (5, 8):
        scratch.append(pltpu.SMEM(operands[position].shape, operands[position].dtype))
    scratch += [
        pltpu.VMEM((layers, foot * sub_dev, LANES), jnp.int32),
        pltpu.VMEM((layers, foot * sub_dev, pixels), jnp.bfloat16),
        pltpu.VMEM((layers, foot * sub_dev, reach), jnp.bfloat16),
        pltpu.VMEM((rowblk, nonzero, acts * comps // SUBLANES, SUBLANES, cbs), jnp.float32),
        pltpu.VMEM((tiles, comps * per_dev, cbs), jnp.float32),
        pltpu.VMEM((tiles * per_dev, SUBLANES, cbs), jnp.float32),
        pltpu.VMEM((grps, rows, LANES), jnp.float32),
        pltpu.VMEM((devices, 1, LANES), jnp.float32),
        pltpu.SemaphoreType.DMA((9,)),
        pltpu.SemaphoreType.DMA((layers,)),
        pltpu.SemaphoreType.DMA((layers, 2)),
        pltpu.SemaphoreType.DMA((layers, 2)),
        pltpu.SemaphoreType.DMA((tiles,)),
        pltpu.SemaphoreType.DMA((tiles,)),
        pltpu.SemaphoreType.DMA((grps,)),
        pltpu.SemaphoreType.DMA((grps,)),
        pltpu.SemaphoreType.DMA((1,)),
        pltpu.SemaphoreType.DMA((1,)),
    ]
    slopes, commands = pl.pallas_call(
        functools.partial(step_kernel, grps, tiles),
        out_shape=(
            pltpu.VMEM((comps, sub_dev), jnp.float32),
            pltpu.VMEM((rows, LANES), jnp.float32),
        ),
        in_specs=[pl.BlockSpec(memory_space=pl.ANY)] * len(operands),
        out_specs=(
            pl.BlockSpec(memory_space=pltpu.VMEM),
            pl.BlockSpec(memory_space=pltpu.VMEM),
        ),
        scratch_shapes=scratch,
        compiler_params=pltpu.CompilerParams(
            collective_id=0, has_side_effects=True, vmem_limit_bytes=56 * 1024 * 1024
        ),
    )(*operands)
    return (slopes, commands.reshape(-1)[:act_dev])


def solution(mesh):
    in_specs = (
        P(None, ("grp", "tile"), None),
        P(),
        P(("grp", "tile"), None, None),
        P(("grp", "tile"), None),
        P("tile", "grp", None, None, None),
        P("tile", "grp"),
        P("tile"),
        P("tile"),
        P(),
    )
    out_specs = (P(None, ("grp", "tile")), P("tile"))
    return jax.shard_map(
        on_device, mesh=mesh, in_specs=in_specs, out_specs=out_specs, check_vma=False
    )
```

```python
import functools
import math

import jax
import jax.numpy as jnp
import numpy as np
from jax import lax
from jax.experimental import pallas as pl
from jax.experimental.pallas import tpu as pltpu
from jax.sharding import PartitionSpec as P

SIDE = 16
LANES = 128
SUBLANES = 8
PIECES = 2
MESH = pl.DeviceIdType.MESH


def transform_table(side):
    index = np.arange(side * side)
    row_ids, col_ids = index // side, index % side
    turns = (row_ids[:, None] * row_ids[None, :] + col_ids[:, None] * col_ids[None, :]) % side
    angle = turns.astype(np.float32) * np.float32(2.0 * math.pi / side)
    cosine, sine = np.cos(angle), np.sin(angle)
    table = np.concatenate(
        [np.concatenate([cosine, -sine], 1), np.concatenate([sine, cosine], 1)], 0
    )
    return jnp.asarray(table.T.astype(jnp.bfloat16))


def cos_sin(x):
    turns = jnp.floor(x * np.float32(2.0 / math.pi) + 0.5)
    r = x - turns * np.float32(1.5703125)
    r = r - turns * np.float32(4.837512969970703125e-4)
    r = r - turns * np.float32(7.54978995489188216e-8)
    r2 = r * r
    s = np.float32(8.3321608736e-3) + r2 * np.float32(-1.9515295891e-4)
    s = np.float32(-1.6666654611e-1) + r2 * s
    s = r + r * r2 * s
    c = np.float32(-1.388731625493765e-3) + r2 * np.float32(2.443315711809948e-5)
    c = np.float32(4.166664568298827e-2) + r2 * c
    c = (1.0 - 0.5 * r2) + r2 * r2 * c
    quarter = turns.astype(jnp.int32)
    odd = (quarter & 1) == 1
    cosine = jnp.where(odd, s, c)
    sine = jnp.where(odd, c, s)
    cosine = jnp.where(((quarter + 1) & 2) == 2, -cosine, cosine)
    sine = jnp.where((quarter & 2) == 2, -sine, sine)
    return cosine, sine


def one_hot(ids, base, width):
    lane = lax.broadcasted_iota(jnp.int32, ids.shape, 1) + base
    hot = [jnp.where(ids == lane + first, 1.0, 0.0) for first in range(0, width, LANES)]
    return jnp.concatenate(hot, 1).astype(jnp.bfloat16)


def ring(start, offset, size):
    place = start + offset
    place = jnp.where(place >= size, place - size, place)
    return jnp.where(place >= size, place - size, place)


def step_kernel(
    grps,
    tiles,
    screens,
    weights,
    footprint,
    illum,
    cm,
    cols,
    prev,
    owner,
    gain,
    table,
    slopes_out,
    commands_out,
    screens_v,
    halo,
    weights_v,
    foot_v,
    illum_v,
    cm_v,
    prev_v,
    owner_v,
    table_v,
    cols_s,
    gain_s,
    ids_v,
    asked,
    asked_v,
    answer_out,
    answer_in,
    picked,
    wide_cm,
    words,
    blocks,
    parts,
    sums,
    load_sem,
    screen_sem,
    halo_send,
    halo_recv,
    ask_send,
    ask_recv,
    answer_send,
    answer_recv,
    word_send,
    word_recv,
    part_send,
    part_recv,
    sum_send,
    sum_recv,
):
    layers, blk_dev, pixels = screens.shape
    foot = footprint.shape[1]
    sub_dev = illum.shape[0]
    reach = halo.shape[1]
    mirrors = gain.shape[0]
    per_dev = sub_dev // LANES
    rowblk, nonzero, tall = wide_cm.shape[:3]
    acts = tall * SUBLANES // 2
    rows = prev.shape[0]
    per_row = LANES // acts
    devices = grps * tiles
    my_grp = lax.axis_index("grp")
    my_tile = lax.axis_index("tile")
    me = my_grp * tiles + my_tile
    odd = lax.rem(me, 2)
    grp_peers = [ring(my_grp, offset, grps) for offset in range(grps)]
    tile_peers = [ring(my_tile, offset, tiles) for offset in range(tiles)]
    everyone = [(g, t) for t in tile_peers for g in grp_peers][1:]

    barrier = pltpu.get_barrier_semaphore()
    for peer in everyone:
        pl.semaphore_signal(barrier, inc=1, device_id=peer, device_id_type=MESH)

    loads = {}
    for number, (name, src, dst) in enumerate(
        [
            ("foot", footprint, foot_v),
            ("weights", weights, weights_v),
            ("cols", cols, cols_s),
            ("gain", gain, gain_s),
            ("prev", prev, prev_v),
            ("owner", owner, owner_v),
            ("illum", illum, illum_v),
            ("table", table, table_v),
            ("cm", cm, cm_v),
        ]
    ):
        loads[name] = pltpu.make_async_copy(src, dst, load_sem.at[number])
    screen_loads = [
        pltpu.make_async_copy(screens.at[layer], screens_v.at[layer], screen_sem.at[layer])
        for layer in range(layers)
    ]
    loads["foot"].start()
    for load in screen_loads:
        load.start()
    for name in loads:
        if name != "foot":
            loads[name].start()

    pl.semaphore_wait(barrier, devices - 1)

    edge = blk_dev - reach

    def beside(step):
        tile = my_tile + step
        turn = jnp.where(tile >= tiles, 1, jnp.where(tile < 0, -1, 0))
        return (ring(my_grp + turn, grps, grps), tile - turn * tiles)

    far_place, near_place = beside(2 * odd - 1), beside(1 - 2 * odd)
    ask = pltpu.make_async_remote_copy(
        src_ref=footprint,
        dst_ref=asked,
        send_sem=ask_send.at[0],
        recv_sem=ask_recv.at[0],
        device_id=far_place,
        device_id_type=MESH,
    )
    ask.start()
    near_copies = []
    for layer in range(layers):
        copy = pltpu.make_async_remote_copy(
            src_ref=screens.at[layer, pl.ds(pl.multiple_of(edge * (1 - odd), reach), reach)],
            dst_ref=halo.at[layer],
            send_sem=halo_send.at[layer],
            recv_sem=halo_recv.at[layer],
            device_id=near_place,
            device_id_type=MESH,
        )
        copy.start()
        near_copies.append(copy)

    loads["foot"].wait()
    for layer in range(layers):
        local = foot_v[layer] - (me * blk_dev - reach)
        local = jnp.where(local < 0, local + blk_dev * devices, local)
        local = jnp.where(local >= blk_dev * devices, local - blk_dev * devices, local)
        flipped = jnp.transpose(local)
        for k in range(foot):
            ids_v[layer, k * sub_dev : (k + 1) * sub_dev, :] = jnp.broadcast_to(
                flipped[:, k : k + 1], (sub_dev, LANES)
            )

    def pick(ids, base, blocks_ref):
        hot = one_hot(ids, base, blocks_ref.shape[0])
        return jnp.dot(hot, blocks_ref[...], preferred_element_type=jnp.float32).astype(
            jnp.bfloat16
        )

    def pick_own(layer):
        picked[layer] = pick(ids_v[layer], reach, screens_v.at[layer, pl.ds(0, reach)])
        for first in range(reach, blk_dev, reach):
            own = screens_v.at[layer, pl.ds(first, reach)]
            picked[layer] += pick(ids_v[layer], reach + first, own)

    def weigh(layer, found):
        count = found.shape[0] // foot
        side_by_side = jnp.concatenate(
            [found[k * count : (k + 1) * count] for k in range(foot)], 1
        )
        own_weights = weights_v[layer * foot : (layer + 1) * foot]
        return jnp.dot(
            side_by_side,
            own_weights.reshape(foot * pixels, pixels),
            preferred_element_type=jnp.float32,
        )

    screen_loads[0].wait()
    pick_own(0)

    ask.wait_recv()
    pieces, piece = asked_v.shape[1], asked_v.shape[2] // foot
    for layer in range(layers):
        flipped = jnp.transpose(asked[layer])
        for k in range(foot):
            for p in range(pieces):
                asked_v[layer, p, k * piece : (k + 1) * piece, :] = jnp.broadcast_to(
                    flipped[p * piece : (p + 1) * piece, k : k + 1], (piece, LANES)
                )
    first_edge = pl.multiple_of(edge * odd, reach)
    loads["weights"].wait()
    for layer in range(1, layers):
        screen_loads[layer].wait()
    answers = []
    for p in range(pieces):
        share = jnp.zeros((piece, pixels), jnp.float32)
        for layer in range(layers):
            at_edge = screens_v.at[layer, pl.ds(first_edge, reach)]
            share += weigh(layer, pick(asked_v[layer, p], me * blk_dev + first_edge, at_edge))
        answer_out[p] = share
        answer = pltpu.make_async_remote_copy(
            src_ref=answer_out.at[p],
            dst_ref=answer_in.at[p],
            send_sem=answer_send.at[p],
            recv_sem=answer_recv.at[p],
            device_id=far_place,
            device_id_type=MESH,
        )
        answer.start()
        answers.append(answer)

    for layer in range(1, layers):
        pick_own(layer)
    near_base = (1 - odd) * (reach + blk_dev)
    phase = jnp.zeros((sub_dev, pixels), jnp.float32)
    for layer in range(layers):
        near_copies[layer].wait_recv()
        phase += weigh(layer, picked[layer] + pick(ids_v[layer], near_base, halo.at[layer]))

    for name in ("cols", "gain", "owner", "prev", "illum", "table"):
        loads[name].wait()
    owners = owner_v[...]
    previous = prev_v[...]
    gains = jnp.zeros(owners.shape, jnp.float32)
    for m in range(mirrors):
        gains = jnp.where(owners == m, gain_s[m], gains)
    first_grp = jnp.where(my_grp == 0, 1.0, 0.0).astype(jnp.float32)

    for answer in answers:
        answer.wait_recv()
    phase += answer_in[...].reshape(sub_dev, pixels)
    cosine, sine = cos_sin(phase)
    bright = illum_v[...]
    field = jnp.concatenate([bright * cosine, bright * sine], 1).astype(jnp.bfloat16)
    spectrum = lax.dot_general(
        table_v[...], field, (((1,), (1,)), ((), ())), preferred_element_type=jnp.float32
    )
    real_part, imag_part = spectrum[:pixels], spectrum[pixels:]
    intensity = real_part * real_part + imag_part * imag_part
    half = SIDE // 2
    wave = lax.broadcasted_iota(jnp.int32, (half, sub_dev), 0).astype(jnp.float32)
    low_v = jnp.zeros((half, sub_dev), jnp.float32)
    high_v = jnp.zeros((half, sub_dev), jnp.float32)
    moment_u = jnp.zeros((half, sub_dev), jnp.float32)
    for u in range(SIDE):
        low = intensity[u * SIDE : u * SIDE + half]
        high = intensity[u * SIDE + half : (u + 1) * SIDE]
        low_v, high_v = low_v + low, high_v + high
        centre_u = float(u - SIDE * (u >= half))
        moment_u = moment_u + centre_u * (low + high)
    moment_v = wave * low_v + (wave - half) * high_v
    total = jnp.sum(low_v + high_v, axis=0, keepdims=True)
    slope_x = jnp.sum(moment_v, axis=0, keepdims=True) / total
    slope_y = jnp.sum(moment_u, axis=0, keepdims=True) / total
    for c, slope in enumerate((slope_x, slope_y)):
        for b in range(per_dev):
            word = slope[:, b * LANES : (b + 1) * LANES].astype(jnp.bfloat16)
            words[my_tile, pl.ds(c * per_dev + b, 1), :] = word.astype(jnp.float32)

    word_copies = []
    for offset in range(1, tiles):
        copy = pltpu.make_async_remote_copy(
            src_ref=words.at[my_tile],
            dst_ref=words.at[my_tile],
            send_sem=word_send.at[offset],
            recv_sem=word_recv.at[offset],
            device_id=(my_grp, tile_peers[offset]),
            device_id_type=MESH,
        )
        copy.start()
        word_copies.append(copy)
    slopes_out[0:1, :] = slope_x
    slopes_out[1:2, :] = slope_y
    loads["cm"].wait()
    for i in range(rowblk):
        wide_cm[i] = cm_v[i].astype(jnp.float32).reshape(wide_cm.shape[1:])
    for copy in word_copies:
        copy.wait_recv()

    x_row = lax.broadcasted_iota(jnp.int32, (SUBLANES, LANES), 0) % 2 == 0
    for d in range(tiles):
        for b in range(per_dev):
            blocks[d * per_dev + b] = jnp.where(
                x_row,
                jnp.broadcast_to(words[d, b : b + 1, :], x_row.shape),
                jnp.broadcast_to(words[d, per_dev + b : per_dev + b + 1, :], x_row.shape),
            )

    base_col = my_grp * (tiles * per_dev)
    act_row = (
        lax.broadcasted_iota(jnp.int32, (tall, SUBLANES, LANES), 0) * SUBLANES
        + lax.broadcasted_iota(jnp.int32, (tall, SUBLANES, LANES), 1)
    ) // 2
    lane = lax.broadcasted_iota(jnp.int32, (tall, SUBLANES, LANES), 2)
    for row in range(rows):
        spread = jnp.zeros((tall, SUBLANES, LANES), jnp.float32)
        for r in range(min(per_row, rowblk - row * per_row)):
            i = row * per_row + r
            products = jnp.zeros((tall, SUBLANES, LANES), jnp.float32)
            for n in range(nonzero):
                block = blocks[jnp.maximum(cols_s[n, i] - base_col, 0)]
                products = products + wide_cm[i, n] * block[None]
            reduced = jnp.sum(products, axis=2, keepdims=True)
            spread = jnp.where(lane == r * acts + act_row, reduced, spread)
        line = jnp.sum(jnp.sum(spread, axis=0), axis=0, keepdims=True)
        parts[my_grp, row : row + 1, :] = line
    partial = parts[my_grp]

    moved = first_grp * previous - gains * partial
    sum_lane = lax.broadcasted_iota(jnp.int32, sums.shape[1:], 1)
    packed = jnp.zeros(sums.shape[1:], jnp.float32)
    for m in range(mirrors):
        amount = jnp.sum(jnp.where(owners == m, moved, 0.0), axis=0, keepdims=True)
        number = jnp.sum(jnp.where(owners == m, first_grp, 0.0), axis=0, keepdims=True)
        packed = jnp.where(sum_lane == m, jnp.sum(amount, axis=1, keepdims=True), packed)
        packed = jnp.where(
            sum_lane == mirrors + m, jnp.sum(number, axis=1, keepdims=True), packed
        )
    sums[me] = packed

    part_copies = []
    for offset in range(1, grps):
        copy = pltpu.make_async_remote_copy(
            src_ref=parts.at[my_grp],
            dst_ref=parts.at[my_grp],
            send_sem=part_send.at[offset],
            recv_sem=part_recv.at[offset],
            device_id=(grp_peers[offset], my_tile),
            device_id_type=MESH,
        )
        copy.start()
        part_copies.append(copy)

    for peer in everyone:
        pltpu.make_async_remote_copy(
            src_ref=sums.at[me],
            dst_ref=sums.at[me],
            send_sem=sum_send.at[0],
            recv_sem=sum_recv.at[0],
            device_id=peer,
            device_id_type=MESH,
        ).start()
    others = sums.at[pl.ds(0, devices - 1)]
    for copy in part_copies:
        copy.wait_recv()
    recon = parts[0]
    for g in range(1, grps):
        recon = recon + parts[g]
    updated = previous - gains * recon
    pltpu.make_async_copy(others, others, sum_recv.at[0]).wait()
    everything = jnp.sum(sums[...], axis=0)
    piston = jnp.zeros(owners.shape, jnp.float32)
    for m in range(mirrors):
        mean = everything[:, m : m + 1] / everything[:, mirrors + m : mirrors + m + 1]
        piston = jnp.where(owners == m, mean, piston)
    commands_out[...] = updated - piston

    for copy in [ask] + answers + near_copies + word_copies + part_copies:
        copy.wait_send()
    pltpu.make_async_copy(others, others, sum_send.at[0]).wait()


def on_device(
    screens,
    interp_weights,
    footprint,
    illumination,
    cm_values,
    cm_columns,
    prev_commands,
    owner_map,
    dm_gain,
):
    grps, tiles = lax.axis_size("grp"), lax.axis_size("tile")
    devices = grps * tiles
    layers, blk_dev, pixels = screens.shape
    sub_dev = illumination.shape[0]
    foot = footprint.shape[2]
    reach = blk_dev // 4
    rowblk, nonzero, acts, comps, cbs = cm_values.shape
    width = nonzero * acts * comps
    act_dev = prev_commands.shape[0]
    mirrors = dm_gain.shape[0]
    per_dev = sub_dev // cbs
    rows = -(-act_dev // LANES)
    spare = rows * LANES - act_dev
    if spare:
        prev_commands = jnp.pad(prev_commands, (0, spare))
        owner_map = jnp.pad(owner_map, (0, spare), constant_values=-1)
    operands = (
        screens,
        interp_weights.reshape(layers * foot, pixels, pixels),
        jnp.transpose(footprint, (1, 2, 0)),
        illumination,
        cm_values.reshape(rowblk, width, cbs),
        jnp.transpose(cm_columns),
        prev_commands.reshape(rows, LANES),
        owner_map.reshape(rows, LANES),
        dm_gain,
        transform_table(SIDE),
    )
    scratch = [pltpu.VMEM(screens.shape, screens.dtype)]
    scratch.append(pltpu.VMEM((layers, reach, pixels), screens.dtype))
    for position in (1, 2, 3, 4, 6, 7, 9):
        scratch.append(pltpu.VMEM(operands[position].shape, operands[position].dtype))
    for position in (5, 8):
        scratch.append(pltpu.SMEM(operands[position].shape, operands[position].dtype))
    scratch += [
        pltpu.VMEM((layers, foot * sub_dev, LANES), jnp.int32),
        pltpu.VMEM((layers, foot, sub_dev), jnp.int32),
        pltpu.VMEM((layers, PIECES, foot * sub_dev // PIECES, LANES), jnp.int32),
        pltpu.VMEM((PIECES, sub_dev // PIECES, pixels), jnp.float32),
        pltpu.VMEM((PIECES, sub_dev // PIECES, pixels), jnp.float32),
        pltpu.VMEM((layers, foot * sub_dev, pixels), jnp.bfloat16),
        pltpu.VMEM((rowblk, nonzero, acts * comps // SUBLANES, SUBLANES, cbs), jnp.float32),
        pltpu.VMEM((tiles, comps * per_dev, cbs), jnp.float32),
        pltpu.VMEM((tiles * per_dev, SUBLANES, cbs), jnp.float32),
        pltpu.VMEM((grps, rows, LANES), jnp.float32),
        pltpu.VMEM((devices, 1, LANES), jnp.float32),
        pltpu.SemaphoreType.DMA((9,)),
        pltpu.SemaphoreType.DMA((layers,)),
        pltpu.SemaphoreType.DMA((layers,)),
        pltpu.SemaphoreType.DMA((layers,)),
        pltpu.SemaphoreType.DMA((1,)),
        pltpu.SemaphoreType.DMA((1,)),
        pltpu.SemaphoreType.DMA((PIECES,)),
        pltpu.SemaphoreType.DMA((PIECES,)),
        pltpu.SemaphoreType.DMA((tiles,)),
        pltpu.SemaphoreType.DMA((tiles,)),
        pltpu.SemaphoreType.DMA((grps,)),
        pltpu.SemaphoreType.DMA((grps,)),
        pltpu.SemaphoreType.DMA((1,)),
        pltpu.SemaphoreType.DMA((1,)),
    ]
    slopes, commands = pl.pallas_call(
        functools.partial(step_kernel, grps, tiles),
        out_shape=(
            pltpu.VMEM((comps, sub_dev), jnp.float32),
            pltpu.VMEM((rows, LANES), jnp.float32),
        ),
        in_specs=[pl.BlockSpec(memory_space=pl.ANY)] * len(operands),
        out_specs=(
            pl.BlockSpec(memory_space=pltpu.VMEM),
            pl.BlockSpec(memory_space=pltpu.VMEM),
        ),
        scratch_shapes=scratch,
        compiler_params=pltpu.CompilerParams(
            collective_id=0, has_side_effects=True, vmem_limit_bytes=56 * 1024 * 1024
        ),
    )(*operands)
    return (slopes, commands.reshape(-1)[:act_dev])


def solution(mesh):
    in_specs = (
        P(None, ("grp", "tile"), None),
        P(),
        P(("grp", "tile"), None, None),
        P(("grp", "tile"), None),
        P("tile", "grp", None, None, None),
        P("tile", "grp"),
        P("tile"),
        P("tile"),
        P(),
    )
    out_specs = (P(None, ("grp", "tile")), P("tile"))
    return jax.shard_map(
        on_device, mesh=mesh, in_specs=in_specs, out_specs=out_specs, check_vma=False
    )
```

```python
import functools
import math

import jax
import jax.numpy as jnp
import numpy as np
from jax import lax
from jax.experimental import pallas as pl
from jax.experimental.pallas import tpu as pltpu
from jax.sharding import PartitionSpec as P

SIDE = 16
LANES = 128
SUBLANES = 8
MESH = pl.DeviceIdType.MESH


def transform_table(side):
    index = np.arange(side * side)
    row_ids, col_ids = index // side, index % side
    turns = (row_ids[:, None] * row_ids[None, :] + col_ids[:, None] * col_ids[None, :]) % side
    angle = turns.astype(np.float32) * np.float32(2.0 * math.pi / side)
    cosine, sine = np.cos(angle), np.sin(angle)
    table = np.concatenate(
        [np.concatenate([cosine, -sine], 1), np.concatenate([sine, cosine], 1)], 0
    )
    return jnp.asarray(table.T.astype(jnp.bfloat16))


def cos_sin(x):
    turns = jnp.floor(x * np.float32(2.0 / math.pi) + 0.5)
    r = x - turns * np.float32(1.5703125)
    r = r - turns * np.float32(4.837512969970703125e-4)
    r = r - turns * np.float32(7.54978995489188216e-8)
    r2 = r * r
    s = np.float32(8.3321608736e-3) + r2 * np.float32(-1.9515295891e-4)
    s = np.float32(-1.6666654611e-1) + r2 * s
    s = r + r * r2 * s
    c = np.float32(-1.388731625493765e-3) + r2 * np.float32(2.443315711809948e-5)
    c = np.float32(4.166664568298827e-2) + r2 * c
    c = (1.0 - 0.5 * r2) + r2 * r2 * c
    quarter = turns.astype(jnp.int32)
    odd = (quarter & 1) == 1
    cosine = jnp.where(odd, s, c)
    sine = jnp.where(odd, c, s)
    cosine = jnp.where(((quarter + 1) & 2) == 2, -cosine, cosine)
    sine = jnp.where((quarter & 2) == 2, -sine, sine)
    return cosine, sine


def one_hot(ids, base, width):
    lane = lax.broadcasted_iota(jnp.int32, ids.shape, 1) + base
    hot = [jnp.where(ids == lane + first, 1.0, 0.0) for first in range(0, width, LANES)]
    return jnp.concatenate(hot, 1).astype(jnp.bfloat16)


def ring(start, offset, size):
    place = start + offset
    place = jnp.where(place >= size, place - size, place)
    return jnp.where(place >= size, place - size, place)


def step_kernel(
    grps,
    tiles,
    screens,
    weights,
    footprint,
    illum,
    cm,
    cols,
    prev,
    owner,
    gain,
    table,
    slopes_out,
    commands_out,
    screens_v,
    halo,
    weights_v,
    foot_v,
    illum_v,
    cm_v,
    prev_v,
    owner_v,
    table_v,
    cols_s,
    gain_s,
    ids_v,
    picked,
    far_hot,
    both_cm,
    wide_cm,
    words,
    blocks,
    parts,
    sums,
    load_sem,
    screen_sem,
    halo_send,
    halo_recv,
    word_send,
    word_recv,
    part_send,
    part_recv,
    sum_send,
    sum_recv,
):
    layers, blk_dev, pixels = screens.shape
    foot = footprint.shape[1]
    sub_dev = illum.shape[0]
    reach = halo.shape[2]
    mirrors = gain.shape[0]
    per_dev = sub_dev // LANES
    rowblk, _, nonzero, tall = wide_cm.shape[:4]
    acts = tall * SUBLANES
    rows = prev.shape[0]
    per_row = LANES // acts
    devices = grps * tiles
    my_grp = lax.axis_index("grp")
    my_tile = lax.axis_index("tile")
    me = my_grp * tiles + my_tile
    odd = lax.rem(me, 2)
    grp_peers = [ring(my_grp, offset, grps) for offset in range(grps)]
    tile_peers = [ring(my_tile, offset, tiles) for offset in range(tiles)]
    steps = [(a, b) for b in range(tiles) for a in range(grps)][1:]
    steps.sort(key=lambda step: (min(step[1], tiles - step[1]) != 1, step[0]))
    everyone = [(grp_peers[a], tile_peers[b]) for a, b in steps]

    barrier = pltpu.get_barrier_semaphore()
    for peer in everyone:
        pl.semaphore_signal(barrier, inc=1, device_id=peer, device_id_type=MESH)

    loads = {}
    for number, (name, src, dst) in enumerate(
        [
            ("foot", footprint, foot_v),
            ("weights", weights, weights_v),
            ("cols", cols, cols_s),
            ("gain", gain, gain_s),
            ("prev", prev, prev_v),
            ("owner", owner, owner_v),
            ("illum", illum, illum_v),
            ("table", table, table_v),
            ("cm", cm, cm_v),
        ]
    ):
        loads[name] = pltpu.make_async_copy(src, dst, load_sem.at[number])
    screen_loads = [
        pltpu.make_async_copy(screens.at[layer], screens_v.at[layer], screen_sem.at[layer])
        for layer in range(layers)
    ]
    loads["foot"].start()
    for load in screen_loads:
        load.start()
    for name in loads:
        if name != "foot":
            loads[name].start()

    pl.semaphore_wait(barrier, devices - 1)

    edge = blk_dev - reach
    far_copies, near_copies = [], []
    for kind, copies in enumerate((far_copies, near_copies)):
        ahead = odd if kind == 0 else 1 - odd
        tile = my_tile + 2 * ahead - 1
        turn = jnp.where(tile >= tiles, 1, jnp.where(tile < 0, -1, 0))
        target = (ring(my_grp + turn, grps, grps), tile - turn * tiles)
        for layer in range(layers):
            copy = pltpu.make_async_remote_copy(
                src_ref=screens.at[layer, pl.ds(pl.multiple_of(edge * ahead, reach), reach)],
                dst_ref=halo.at[layer, kind],
                send_sem=halo_send.at[layer, kind],
                recv_sem=halo_recv.at[layer, kind],
                device_id=target,
                device_id_type=MESH,
            )
            copy.start()
            copies.append(copy)

    loads["foot"].wait()
    for layer in range(layers):
        local = foot_v[layer] - (me * blk_dev - reach)
        local = jnp.where(local < 0, local + blk_dev * devices, local)
        local = jnp.where(local >= blk_dev * devices, local - blk_dev * devices, local)
        flipped = jnp.transpose(local)
        for k in range(foot):
            ids_v[layer, k * sub_dev : (k + 1) * sub_dev, :] = jnp.broadcast_to(
                flipped[:, k : k + 1], (sub_dev, LANES)
            )

    def pick(layer, base, blocks_ref):
        hot = one_hot(ids_v[layer], base, blocks_ref.shape[0])
        return jnp.dot(hot, blocks_ref[...], preferred_element_type=jnp.float32).astype(
            jnp.bfloat16
        )

    def weigh(layer, found):
        side_by_side = jnp.concatenate(
            [found[k * sub_dev : (k + 1) * sub_dev] for k in range(foot)], 1
        )
        own_weights = weights_v[layer * foot : (layer + 1) * foot]
        return jnp.dot(
            side_by_side,
            own_weights.reshape(foot * pixels, pixels),
            preferred_element_type=jnp.float32,
        )

    for layer in range(layers):
        screen_loads[layer].wait()
        picked[layer] = pick(layer, reach, screens_v.at[layer, pl.ds(0, reach)])
        for first in range(reach, blk_dev, reach):
            picked[layer] += pick(layer, reach + first, screens_v.at[layer, pl.ds(first, reach)])

    past = reach + blk_dev
    far_base, near_base = odd * past, (1 - odd) * past
    loads["weights"].wait()
    phase = jnp.zeros((sub_dev, pixels), jnp.float32)
    for layer in range(layers):
        near_copies[layer].wait_recv()
        phase += weigh(layer, picked[layer] + pick(layer, near_base, halo.at[layer, 1]))
    for layer in range(layers):
        far_hot[layer] = one_hot(ids_v[layer], far_base, reach)

    loads["cm"].wait()
    for i in range(rowblk):
        both_cm[i] = cm_v[i].astype(jnp.float32)
    for i in range(rowblk):
        for c in range(2):
            own = both_cm[i, pl.ds(c, nonzero * acts, stride=2), :]
            wide_cm[i, c] = own.reshape(wide_cm.shape[2:])

    for name in ("cols", "gain", "owner", "prev", "illum", "table"):
        loads[name].wait()
    owners = owner_v[...]
    previous = prev_v[...]
    gains = jnp.zeros(owners.shape, jnp.float32)
    for m in range(mirrors):
        gains = jnp.where(owners == m, gain_s[m], gains)
    first_grp = jnp.where(my_grp == 0, 1.0, 0.0).astype(jnp.float32)

    for layer in range(layers):
        far_copies[layer].wait_recv()
        other = jnp.dot(far_hot[layer], halo[layer, 0], preferred_element_type=jnp.float32)
        phase += weigh(layer, other.astype(jnp.bfloat16))

    cosine, sine = cos_sin(phase)
    bright = illum_v[...]
    field = jnp.concatenate([bright * cosine, bright * sine], 1).astype(jnp.bfloat16)
    spectrum = lax.dot_general(
        table_v[...], field, (((1,), (1,)), ((), ())), preferred_element_type=jnp.float32
    )
    real_part, imag_part = spectrum[:pixels], spectrum[pixels:]
    intensity = real_part * real_part + imag_part * imag_part
    half = SIDE // 2
    wave = lax.broadcasted_iota(jnp.int32, (half, sub_dev), 0).astype(jnp.float32)
    low_v = jnp.zeros((half, sub_dev), jnp.float32)
    high_v = jnp.zeros((half, sub_dev), jnp.float32)
    moment_u = jnp.zeros((half, sub_dev), jnp.float32)
    for u in range(SIDE):
        low = intensity[u * SIDE : u * SIDE + half]
        high = intensity[u * SIDE + half : (u + 1) * SIDE]
        low_v, high_v = low_v + low, high_v + high
        centre_u = float(u - SIDE * (u >= half))
        moment_u = moment_u + centre_u * (low + high)
    moment_v = wave * low_v + (wave - half) * high_v
    total = jnp.sum(low_v + high_v, axis=0, keepdims=True)
    slope_x = jnp.sum(moment_v, axis=0, keepdims=True) / total
    slope_y = jnp.sum(moment_u, axis=0, keepdims=True) / total
    for c, slope in enumerate((slope_x, slope_y)):
        for b in range(per_dev):
            word = slope[:, b * LANES : (b + 1) * LANES].astype(jnp.bfloat16)
            words[my_tile, pl.ds(c * per_dev + b, 1), :] = word.astype(jnp.float32)

    word_copies = []
    for offset in range(1, tiles):
        copy = pltpu.make_async_remote_copy(
            src_ref=words.at[my_tile],
            dst_ref=words.at[my_tile],
            send_sem=word_send.at[offset],
            recv_sem=word_recv.at[offset],
            device_id=(my_grp, tile_peers[offset]),
            device_id_type=MESH,
        )
        copy.start()
        word_copies.append(copy)
    slopes_out[0:1, :] = slope_x
    slopes_out[1:2, :] = slope_y
    for copy in word_copies:
        copy.wait_recv()

    for d in range(tiles):
        for b in range(per_dev):
            for c in range(2):
                row = words[d, c * per_dev + b : c * per_dev + b + 1, :]
                blocks[d * per_dev + b, c] = jnp.broadcast_to(row, (SUBLANES, LANES))

    base_col = my_grp * (tiles * per_dev)
    act_row = (
        lax.broadcasted_iota(jnp.int32, (tall, SUBLANES, LANES), 0) * SUBLANES
        + lax.broadcasted_iota(jnp.int32, (tall, SUBLANES, LANES), 1)
    )
    lane = lax.broadcasted_iota(jnp.int32, (tall, SUBLANES, LANES), 2)
    for row in range(rows):
        spread = jnp.zeros((tall, SUBLANES, LANES), jnp.float32)
        for r in range(min(per_row, rowblk - row * per_row)):
            i = row * per_row + r
            products = jnp.zeros((tall, SUBLANES, LANES), jnp.float32)
            for n in range(nonzero):
                block = blocks[jnp.maximum(cols_s[n, i] - base_col, 0)]
                for c in range(2):
                    products = products + wide_cm[i, c, n] * block[c][None]
            reduced = jnp.sum(products, axis=2, keepdims=True)
            spread = jnp.where(lane == r * acts + act_row, reduced, spread)
        line = jnp.sum(jnp.sum(spread, axis=0), axis=0, keepdims=True)
        parts[my_grp, row : row + 1, :] = line
    partial = parts[my_grp]

    moved = first_grp * previous - gains * partial
    sum_lane = lax.broadcasted_iota(jnp.int32, sums.shape[1:], 1)
    packed = jnp.zeros(sums.shape[1:], jnp.float32)
    for m in range(mirrors):
        amount = jnp.sum(jnp.where(owners == m, moved, 0.0), axis=0, keepdims=True)
        number = jnp.sum(jnp.where(owners == m, first_grp, 0.0), axis=0, keepdims=True)
        packed = jnp.where(sum_lane == m, jnp.sum(amount, axis=1, keepdims=True), packed)
        packed = jnp.where(
            sum_lane == mirrors + m, jnp.sum(number, axis=1, keepdims=True), packed
        )
    sums[me] = packed

    part_copies = []
    for offset in range(1, grps):
        copy = pltpu.make_async_remote_copy(
            src_ref=parts.at[my_grp],
            dst_ref=parts.at[my_grp],
            send_sem=part_send.at[offset],
            recv_sem=part_recv.at[offset],
            device_id=(grp_peers[offset], my_tile),
            device_id_type=MESH,
        )
        copy.start()
        part_copies.append(copy)

    for peer in everyone:
        pltpu.make_async_remote_copy(
            src_ref=sums.at[me],
            dst_ref=sums.at[me],
            send_sem=sum_send.at[0],
            recv_sem=sum_recv.at[0],
            device_id=peer,
            device_id_type=MESH,
        ).start()
    others = sums.at[pl.ds(0, devices - 1)]
    for copy in part_copies:
        copy.wait_recv()
    recon = parts[0]
    for g in range(1, grps):
        recon = recon + parts[g]
    updated = previous - gains * recon
    pltpu.make_async_copy(others, others, sum_recv.at[0]).wait()
    everything = jnp.sum(sums[...], axis=0)
    piston = jnp.zeros(owners.shape, jnp.float32)
    for m in range(mirrors):
        mean = everything[:, m : m + 1] / everything[:, mirrors + m : mirrors + m + 1]
        piston = jnp.where(owners == m, mean, piston)
    commands_out[...] = updated - piston

    for copy in far_copies + near_copies + word_copies + part_copies:
        copy.wait_send()
    pltpu.make_async_copy(others, others, sum_send.at[0]).wait()


def write_out(slopes, commands, slopes_out, commands_out, sem):
    first = pltpu.make_async_copy(slopes, slopes_out, sem.at[0])
    second = pltpu.make_async_copy(commands, commands_out, sem.at[1])
    first.start()
    second.start()
    first.wait()
    second.wait()


def on_device(
    screens,
    interp_weights,
    footprint,
    illumination,
    cm_values,
    cm_columns,
    prev_commands,
    owner_map,
    dm_gain,
):
    grps, tiles = lax.axis_size("grp"), lax.axis_size("tile")
    devices = grps * tiles
    layers, blk_dev, pixels = screens.shape
    sub_dev = illumination.shape[0]
    foot = footprint.shape[2]
    reach = blk_dev // 4
    rowblk, nonzero, acts, comps, cbs = cm_values.shape
    width = nonzero * acts * comps
    act_dev = prev_commands.shape[0]
    mirrors = dm_gain.shape[0]
    per_dev = sub_dev // cbs
    rows = -(-act_dev // LANES)
    spare = rows * LANES - act_dev
    if spare:
        prev_commands = jnp.pad(prev_commands, (0, spare))
        owner_map = jnp.pad(owner_map, (0, spare), constant_values=-1)
    operands = (
        screens,
        interp_weights.reshape(layers * foot, pixels, pixels),
        jnp.transpose(footprint, (1, 2, 0)),
        illumination,
        cm_values.reshape(rowblk, width, cbs),
        jnp.transpose(cm_columns),
        prev_commands.reshape(rows, LANES),
        owner_map.reshape(rows, LANES),
        dm_gain,
        transform_table(SIDE),
    )
    scratch = [pltpu.VMEM(screens.shape, screens.dtype)]
    scratch.append(pltpu.VMEM((layers, 2, reach, pixels), screens.dtype))
    for position in (1, 2, 3, 4, 6, 7, 9):
        scratch.append(pltpu.VMEM(operands[position].shape, operands[position].dtype))
    for position in (5, 8):
        scratch.append(pltpu.SMEM(operands[position].shape, operands[position].dtype))
    scratch += [
        pltpu.VMEM((layers, foot * sub_dev, LANES), jnp.int32),
        pltpu.VMEM((layers, foot * sub_dev, pixels), jnp.bfloat16),
        pltpu.VMEM((layers, foot * sub_dev, reach), jnp.bfloat16),
        pltpu.VMEM((rowblk, width, cbs), jnp.float32),
        pltpu.VMEM((rowblk, comps, nonzero, acts // SUBLANES, SUBLANES, cbs), jnp.float32),
        pltpu.VMEM((tiles, comps * per_dev, cbs), jnp.float32),
        pltpu.VMEM((tiles * per_dev, comps, SUBLANES, cbs), jnp.float32),
        pltpu.VMEM((grps, rows, LANES), jnp.float32),
        pltpu.VMEM((devices, 1, LANES), jnp.float32),
        pltpu.SemaphoreType.DMA((9,)),
        pltpu.SemaphoreType.DMA((layers,)),
        pltpu.SemaphoreType.DMA((layers, 2)),
        pltpu.SemaphoreType.DMA((layers, 2)),
        pltpu.SemaphoreType.DMA((tiles,)),
        pltpu.SemaphoreType.DMA((tiles,)),
        pltpu.SemaphoreType.DMA((grps,)),
        pltpu.SemaphoreType.DMA((grps,)),
        pltpu.SemaphoreType.DMA((1,)),
        pltpu.SemaphoreType.DMA((1,)),
    ]
    slopes, commands = pl.pallas_call(
        functools.partial(step_kernel, grps, tiles),
        out_shape=(
            pltpu.VMEM((comps, sub_dev), jnp.float32),
            pltpu.VMEM((rows, LANES), jnp.float32),
        ),
        in_specs=[pl.BlockSpec(memory_space=pl.ANY)] * len(operands),
        out_specs=(
            pl.BlockSpec(memory_space=pltpu.VMEM),
            pl.BlockSpec(memory_space=pltpu.VMEM),
        ),
        scratch_shapes=scratch,
        compiler_params=pltpu.CompilerParams(
            collective_id=0, has_side_effects=True, vmem_limit_bytes=56 * 1024 * 1024
        ),
    )(*operands)
    slopes, commands = pl.pallas_call(
        write_out,
        out_shape=(
            jax.ShapeDtypeStruct(slopes.shape, slopes.dtype),
            jax.ShapeDtypeStruct(commands.shape, commands.dtype),
        ),
        in_specs=[pl.BlockSpec(memory_space=pltpu.VMEM)] * 2,
        out_specs=(pl.BlockSpec(memory_space=pltpu.HBM), pl.BlockSpec(memory_space=pltpu.HBM)),
        scratch_shapes=[pltpu.SemaphoreType.DMA((2,))],
    )(
        pltpu.with_memory_space_constraint(slopes, pltpu.VMEM),
        pltpu.with_memory_space_constraint(commands, pltpu.VMEM),
    )
    return (slopes, commands.reshape(-1)[:act_dev])


def solution(mesh):
    in_specs = (
        P(None, ("grp", "tile"), None),
        P(),
        P(("grp", "tile"), None, None),
        P(("grp", "tile"), None),
        P("tile", "grp", None, None, None),
        P("tile", "grp"),
        P("tile"),
        P("tile"),
        P(),
    )
    out_specs = (P(None, ("grp", "tile")), P("tile"))
    return jax.shard_map(
        on_device, mesh=mesh, in_specs=in_specs, out_specs=out_specs, check_vma=False
    )
```

```python
import functools
import math

import jax
import jax.numpy as jnp
import numpy as np
from jax import lax
from jax.experimental import pallas as pl
from jax.experimental.pallas import tpu as pltpu
from jax.sharding import PartitionSpec as P

SIDE = 16
LANES = 128
SUBLANES = 8
MESH = pl.DeviceIdType.MESH


def transform_table(side):
    index = np.arange(side * side)
    row_ids, col_ids = index // side, index % side
    turns = (row_ids[:, None] * row_ids[None, :] + col_ids[:, None] * col_ids[None, :]) % side
    angle = turns.astype(np.float32) * np.float32(2.0 * math.pi / side)
    cosine, sine = np.cos(angle), np.sin(angle)
    table = np.concatenate(
        [np.concatenate([cosine, -sine], 1), np.concatenate([sine, cosine], 1)], 0
    )
    return jnp.asarray(table.T.astype(jnp.bfloat16))


def cos_sin(x):
    turns = jnp.floor(x * np.float32(2.0 / math.pi) + 0.5)
    r = x - turns * np.float32(1.5703125)
    r = r - turns * np.float32(4.837512969970703125e-4)
    r = r - turns * np.float32(7.54978995489188216e-8)
    r2 = r * r
    s = np.float32(8.3321608736e-3) + r2 * np.float32(-1.9515295891e-4)
    s = np.float32(-1.6666654611e-1) + r2 * s
    s = r + r * r2 * s
    c = np.float32(-1.388731625493765e-3) + r2 * np.float32(2.443315711809948e-5)
    c = np.float32(4.166664568298827e-2) + r2 * c
    c = (1.0 - 0.5 * r2) + r2 * r2 * c
    quarter = turns.astype(jnp.int32)
    odd = (quarter & 1) == 1
    cosine = jnp.where(odd, s, c)
    sine = jnp.where(odd, c, s)
    cosine = jnp.where(((quarter + 1) & 2) == 2, -cosine, cosine)
    sine = jnp.where((quarter & 2) == 2, -sine, sine)
    return cosine, sine


def one_hot(ids, base, width):
    lane = lax.broadcasted_iota(jnp.int32, ids.shape, 1) + base
    hot = [jnp.where(ids == lane + first, 1.0, 0.0) for first in range(0, width, LANES)]
    return jnp.concatenate(hot, 1).astype(jnp.bfloat16)


def ring(start, offset, size):
    place = start + offset
    place = jnp.where(place >= size, place - size, place)
    return jnp.where(place >= size, place - size, place)


def step_kernel(
    grps,
    tiles,
    screens,
    weights,
    footprint,
    illum,
    cm,
    cols,
    prev,
    owner,
    gain,
    table,
    slopes_out,
    commands_out,
    screens_v,
    halo,
    weights_v,
    foot_v,
    illum_v,
    cm_v,
    prev_v,
    owner_v,
    table_v,
    cols_s,
    gain_s,
    ids_v,
    picked,
    far_hot,
    both_cm,
    wide_cm,
    words,
    blocks,
    parts,
    sums,
    load_sem,
    screen_sem,
    halo_send,
    halo_recv,
    word_send,
    word_recv,
    part_send,
    part_recv,
    sum_send,
    sum_recv,
):
    layers, blk_dev, pixels = screens.shape
    foot = footprint.shape[1]
    sub_dev = illum.shape[0]
    reach = halo.shape[2]
    mirrors = gain.shape[0]
    per_dev = sub_dev // LANES
    rowblk, _, nonzero, tall = wide_cm.shape[:4]
    acts = tall * SUBLANES
    rows = prev.shape[0]
    per_row = LANES // acts
    devices = grps * tiles
    my_grp = lax.axis_index("grp")
    my_tile = lax.axis_index("tile")
    me = my_grp * tiles + my_tile
    odd = lax.rem(me, 2)
    grp_peers = [ring(my_grp, offset, grps) for offset in range(grps)]
    tile_peers = [ring(my_tile, offset, tiles) for offset in range(tiles)]
    steps = [(a, b) for b in range(tiles) for a in range(grps)][1:]
    steps.sort(key=lambda step: (min(step[1], tiles - step[1]) != 1, step[0]))
    everyone = [(grp_peers[a], tile_peers[b]) for a, b in steps]

    barrier = pltpu.get_barrier_semaphore()
    for peer in everyone:
        pl.semaphore_signal(barrier, inc=1, device_id=peer, device_id_type=MESH)

    loads = {}
    for number, (name, src, dst) in enumerate(
        [
            ("foot", footprint, foot_v),
            ("weights", weights, weights_v),
            ("cols", cols, cols_s),
            ("gain", gain, gain_s),
            ("prev", prev, prev_v),
            ("owner", owner, owner_v),
            ("illum", illum, illum_v),
            ("table", table, table_v),
            ("cm", cm, cm_v),
        ]
    ):
        loads[name] = pltpu.make_async_copy(src, dst, load_sem.at[number])
    screen_loads = [
        pltpu.make_async_copy(screens.at[layer], screens_v.at[layer], screen_sem.at[layer])
        for layer in range(layers)
    ]
    loads["foot"].start()
    for load in screen_loads:
        load.start()
    for name in loads:
        if name != "foot":
            loads[name].start()

    pl.semaphore_wait(barrier, devices - 1)

    edge = blk_dev - reach
    far_copies, near_copies = [], []
    for kind, copies in enumerate((far_copies, near_copies)):
        ahead = odd if kind == 0 else 1 - odd
        tile = my_tile + 2 * ahead - 1
        turn = jnp.where(tile >= tiles, 1, jnp.where(tile < 0, -1, 0))
        target = (ring(my_grp + turn, grps, grps), tile - turn * tiles)
        for piece in range(2 * layers):
            layer, start = piece // 2, (piece % 2) * (reach // 2)
            first = pl.multiple_of(edge * ahead + start, reach // 2)
            copy = pltpu.make_async_remote_copy(
                src_ref=screens.at[layer, pl.ds(first, reach // 2)],
                dst_ref=halo.at[layer, kind, pl.ds(start, reach // 2)],
                send_sem=halo_send.at[piece, kind],
                recv_sem=halo_recv.at[piece, kind],
                device_id=target,
                device_id_type=MESH,
            )
            copy.start()
            copies.append(copy)

    loads["foot"].wait()
    for layer in range(layers):
        local = foot_v[layer] - (me * blk_dev - reach)
        local = jnp.where(local < 0, local + blk_dev * devices, local)
        local = jnp.where(local >= blk_dev * devices, local - blk_dev * devices, local)
        flipped = jnp.transpose(local)
        for k in range(foot):
            ids_v[layer, k * sub_dev : (k + 1) * sub_dev, :] = jnp.broadcast_to(
                flipped[:, k : k + 1], (sub_dev, LANES)
            )

    def pick(layer, base, blocks_ref):
        hot = one_hot(ids_v[layer], base, blocks_ref.shape[0])
        return jnp.dot(hot, blocks_ref[...], preferred_element_type=jnp.float32).astype(
            jnp.bfloat16
        )

    def weigh(layer, found):
        side_by_side = jnp.concatenate(
            [found[k * sub_dev : (k + 1) * sub_dev] for k in range(foot)], 1
        )
        own_weights = weights_v[layer * foot : (layer + 1) * foot]
        return jnp.dot(
            side_by_side,
            own_weights.reshape(foot * pixels, pixels),
            preferred_element_type=jnp.float32,
        )

    for layer in range(layers):
        screen_loads[layer].wait()
        picked[layer] = pick(layer, reach, screens_v.at[layer, pl.ds(0, reach)])
        for first in range(reach, blk_dev, reach):
            picked[layer] += pick(layer, reach + first, screens_v.at[layer, pl.ds(first, reach)])

    past = reach + blk_dev
    far_base, near_base = odd * past, (1 - odd) * past
    loads["weights"].wait()
    phase = jnp.zeros((sub_dev, pixels), jnp.float32)
    for layer in range(layers):
        near_copies[2 * layer].wait_recv()
        near_copies[2 * layer + 1].wait_recv()
        phase += weigh(layer, picked[layer] + pick(layer, near_base, halo.at[layer, 1]))
    for layer in range(layers):
        far_hot[layer] = one_hot(ids_v[layer], far_base, reach)

    loads["cm"].wait()
    for i in range(rowblk):
        both_cm[i] = cm_v[i].astype(jnp.float32)
    for i in range(rowblk):
        for c in range(2):
            own = both_cm[i, pl.ds(c, nonzero * acts, stride=2), :]
            wide_cm[i, c] = own.reshape(wide_cm.shape[2:])

    for name in ("cols", "gain", "owner", "prev", "illum", "table"):
        loads[name].wait()
    owners = owner_v[...]
    previous = prev_v[...]
    gains = jnp.zeros(owners.shape, jnp.float32)
    for m in range(mirrors):
        gains = jnp.where(owners == m, gain_s[m], gains)
    first_grp = jnp.where(my_grp == 0, 1.0, 0.0).astype(jnp.float32)

    for layer in range(layers):
        far_copies[2 * layer].wait_recv()
        far_copies[2 * layer + 1].wait_recv()
        other = jnp.dot(far_hot[layer], halo[layer, 0], preferred_element_type=jnp.float32)
        phase += weigh(layer, other.astype(jnp.bfloat16))

    cosine, sine = cos_sin(phase)
    bright = illum_v[...]
    field = jnp.concatenate([bright * cosine, bright * sine], 1).astype(jnp.bfloat16)
    spectrum = lax.dot_general(
        table_v[...], field, (((1,), (1,)), ((), ())), preferred_element_type=jnp.float32
    )
    real_part, imag_part = spectrum[:pixels], spectrum[pixels:]
    intensity = real_part * real_part + imag_part * imag_part
    half = SIDE // 2
    wave = lax.broadcasted_iota(jnp.int32, (half, sub_dev), 0).astype(jnp.float32)
    low_v = jnp.zeros((half, sub_dev), jnp.float32)
    high_v = jnp.zeros((half, sub_dev), jnp.float32)
    moment_u = jnp.zeros((half, sub_dev), jnp.float32)
    for u in range(SIDE):
        low = intensity[u * SIDE : u * SIDE + half]
        high = intensity[u * SIDE + half : (u + 1) * SIDE]
        low_v, high_v = low_v + low, high_v + high
        centre_u = float(u - SIDE * (u >= half))
        moment_u = moment_u + centre_u * (low + high)
    moment_v = wave * low_v + (wave - half) * high_v
    total = jnp.sum(low_v + high_v, axis=0, keepdims=True)
    slope_x = jnp.sum(moment_v, axis=0, keepdims=True) / total
    slope_y = jnp.sum(moment_u, axis=0, keepdims=True) / total
    for c, slope in enumerate((slope_x, slope_y)):
        for b in range(per_dev):
            word = slope[:, b * LANES : (b + 1) * LANES].astype(jnp.bfloat16)
            words[my_tile, pl.ds(c * per_dev + b, 1), :] = word.astype(jnp.float32)

    word_copies = []
    for offset in range(1, tiles):
        copy = pltpu.make_async_remote_copy(
            src_ref=words.at[my_tile],
            dst_ref=words.at[my_tile],
            send_sem=word_send.at[offset],
            recv_sem=word_recv.at[offset],
            device_id=(my_grp, tile_peers[offset]),
            device_id_type=MESH,
        )
        copy.start()
        word_copies.append(copy)
    slopes_out[0:1, :] = slope_x
    slopes_out[1:2, :] = slope_y
    for copy in word_copies:
        copy.wait_recv()

    for d in range(tiles):
        for b in range(per_dev):
            for c in range(2):
                row = words[d, c * per_dev + b : c * per_dev + b + 1, :]
                blocks[d * per_dev + b, c] = jnp.broadcast_to(row, (SUBLANES, LANES))

    base_col = my_grp * (tiles * per_dev)
    act_row = (
        lax.broadcasted_iota(jnp.int32, (tall, SUBLANES, LANES), 0) * SUBLANES
        + lax.broadcasted_iota(jnp.int32, (tall, SUBLANES, LANES), 1)
    )
    lane = lax.broadcasted_iota(jnp.int32, (tall, SUBLANES, LANES), 2)
    for row in range(rows):
        spread = jnp.zeros((tall, SUBLANES, LANES), jnp.float32)
        for r in range(min(per_row, rowblk - row * per_row)):
            i = row * per_row + r
            products = jnp.zeros((tall, SUBLANES, LANES), jnp.float32)
            for n in range(nonzero):
                block = blocks[jnp.maximum(cols_s[n, i] - base_col, 0)]
                for c in range(2):
                    products = products + wide_cm[i, c, n] * block[c][None]
            reduced = jnp.sum(products, axis=2, keepdims=True)
            spread = jnp.where(lane == r * acts + act_row, reduced, spread)
        line = jnp.sum(jnp.sum(spread, axis=0), axis=0, keepdims=True)
        parts[my_grp, row : row + 1, :] = line
    partial = parts[my_grp]

    moved = first_grp * previous - gains * partial
    sum_lane = lax.broadcasted_iota(jnp.int32, sums.shape[1:], 1)
    packed = jnp.zeros(sums.shape[1:], jnp.float32)
    for m in range(mirrors):
        amount = jnp.sum(jnp.where(owners == m, moved, 0.0), axis=0, keepdims=True)
        number = jnp.sum(jnp.where(owners == m, first_grp, 0.0), axis=0, keepdims=True)
        packed = jnp.where(sum_lane == m, jnp.sum(amount, axis=1, keepdims=True), packed)
        packed = jnp.where(
            sum_lane == mirrors + m, jnp.sum(number, axis=1, keepdims=True), packed
        )
    sums[me] = packed

    part_copies = []
    for offset in range(1, grps):
        copy = pltpu.make_async_remote_copy(
            src_ref=parts.at[my_grp],
            dst_ref=parts.at[my_grp],
            send_sem=part_send.at[offset],
            recv_sem=part_recv.at[offset],
            device_id=(grp_peers[offset], my_tile),
            device_id_type=MESH,
        )
        copy.start()
        part_copies.append(copy)

    for peer in everyone[::-1]:
        pltpu.make_async_remote_copy(
            src_ref=sums.at[me],
            dst_ref=sums.at[me],
            send_sem=sum_send.at[0],
            recv_sem=sum_recv.at[0],
            device_id=peer,
            device_id_type=MESH,
        ).start()
    others = sums.at[pl.ds(0, devices - 1)]
    for copy in part_copies:
        copy.wait_recv()
    recon = parts[0]
    for g in range(1, grps):
        recon = recon + parts[g]
    updated = previous - gains * recon
    pltpu.make_async_copy(others, others, sum_recv.at[0]).wait()
    everything = jnp.sum(sums[...], axis=0)
    piston = jnp.zeros(owners.shape, jnp.float32)
    for m in range(mirrors):
        mean = everything[:, m : m + 1] / everything[:, mirrors + m : mirrors + m + 1]
        piston = jnp.where(owners == m, mean, piston)
    commands_out[...] = updated - piston

    for copy in far_copies + near_copies + word_copies + part_copies:
        copy.wait_send()
    pltpu.make_async_copy(others, others, sum_send.at[0]).wait()


def write_out(slopes, commands, slopes_out, commands_out, sem):
    first = pltpu.make_async_copy(slopes, slopes_out, sem.at[0])
    second = pltpu.make_async_copy(commands, commands_out, sem.at[1])
    first.start()
    second.start()
    first.wait()
    second.wait()


def on_device(
    screens,
    interp_weights,
    footprint,
    illumination,
    cm_values,
    cm_columns,
    prev_commands,
    owner_map,
    dm_gain,
):
    grps, tiles = lax.axis_size("grp"), lax.axis_size("tile")
    devices = grps * tiles
    layers, blk_dev, pixels = screens.shape
    sub_dev = illumination.shape[0]
    foot = footprint.shape[2]
    reach = blk_dev // 4
    rowblk, nonzero, acts, comps, cbs = cm_values.shape
    width = nonzero * acts * comps
    act_dev = prev_commands.shape[0]
    mirrors = dm_gain.shape[0]
    per_dev = sub_dev // cbs
    rows = -(-act_dev // LANES)
    spare = rows * LANES - act_dev
    if spare:
        prev_commands = jnp.pad(prev_commands, (0, spare))
        owner_map = jnp.pad(owner_map, (0, spare), constant_values=-1)
    operands = (
        screens,
        interp_weights.reshape(layers * foot, pixels, pixels),
        jnp.transpose(footprint, (1, 2, 0)),
        illumination,
        cm_values.reshape(rowblk, width, cbs),
        jnp.transpose(cm_columns),
        prev_commands.reshape(rows, LANES),
        owner_map.reshape(rows, LANES),
        dm_gain,
        transform_table(SIDE),
    )
    scratch = [pltpu.VMEM(screens.shape, screens.dtype)]
    scratch.append(pltpu.VMEM((layers, 2, reach, pixels), screens.dtype))
    for position in (1, 2, 3, 4, 6, 7, 9):
        scratch.append(pltpu.VMEM(operands[position].shape, operands[position].dtype))
    for position in (5, 8):
        scratch.append(pltpu.SMEM(operands[position].shape, operands[position].dtype))
    scratch += [
        pltpu.VMEM((layers, foot * sub_dev, LANES), jnp.int32),
        pltpu.VMEM((layers, foot * sub_dev, pixels), jnp.bfloat16),
        pltpu.VMEM((layers, foot * sub_dev, reach), jnp.bfloat16),
        pltpu.VMEM((rowblk, width, cbs), jnp.float32),
        pltpu.VMEM((rowblk, comps, nonzero, acts // SUBLANES, SUBLANES, cbs), jnp.float32),
        pltpu.VMEM((tiles, comps * per_dev, cbs), jnp.float32),
        pltpu.VMEM((tiles * per_dev, comps, SUBLANES, cbs), jnp.float32),
        pltpu.VMEM((grps, rows, LANES), jnp.float32),
        pltpu.VMEM((devices, 1, LANES), jnp.float32),
        pltpu.SemaphoreType.DMA((9,)),
        pltpu.SemaphoreType.DMA((layers,)),
        pltpu.SemaphoreType.DMA((2 * layers, 2)),
        pltpu.SemaphoreType.DMA((2 * layers, 2)),
        pltpu.SemaphoreType.DMA((tiles,)),
        pltpu.SemaphoreType.DMA((tiles,)),
        pltpu.SemaphoreType.DMA((grps,)),
        pltpu.SemaphoreType.DMA((grps,)),
        pltpu.SemaphoreType.DMA((1,)),
        pltpu.SemaphoreType.DMA((1,)),
    ]
    slopes, commands = pl.pallas_call(
        functools.partial(step_kernel, grps, tiles),
        out_shape=(
            pltpu.VMEM((comps, sub_dev), jnp.float32),
            pltpu.VMEM((rows, LANES), jnp.float32),
        ),
        in_specs=[pl.BlockSpec(memory_space=pl.ANY)] * len(operands),
        out_specs=(
            pl.BlockSpec(memory_space=pltpu.VMEM),
            pl.BlockSpec(memory_space=pltpu.VMEM),
        ),
        scratch_shapes=scratch,
        compiler_params=pltpu.CompilerParams(
            collective_id=0, has_side_effects=True, vmem_limit_bytes=56 * 1024 * 1024
        ),
    )(*operands)
    slopes, commands = pl.pallas_call(
        write_out,
        out_shape=(
            jax.ShapeDtypeStruct(slopes.shape, slopes.dtype),
            jax.ShapeDtypeStruct(commands.shape, commands.dtype),
        ),
        in_specs=[pl.BlockSpec(memory_space=pltpu.VMEM)] * 2,
        out_specs=(pl.BlockSpec(memory_space=pltpu.HBM), pl.BlockSpec(memory_space=pltpu.HBM)),
        scratch_shapes=[pltpu.SemaphoreType.DMA((2,))],
    )(
        pltpu.with_memory_space_constraint(slopes, pltpu.VMEM),
        pltpu.with_memory_space_constraint(commands, pltpu.VMEM),
    )
    return (slopes, commands.reshape(-1)[:act_dev])


def solution(mesh):
    in_specs = (
        P(None, ("grp", "tile"), None),
        P(),
        P(("grp", "tile"), None, None),
        P(("grp", "tile"), None),
        P("tile", "grp", None, None, None),
        P("tile", "grp"),
        P("tile"),
        P("tile"),
        P(),
    )
    out_specs = (P(None, ("grp", "tile")), P("tile"))
    return jax.shard_map(
        on_device, mesh=mesh, in_specs=in_specs, out_specs=out_specs, check_vma=False
    )
```
